32 devices in a mesh: dp: 8 (over y, x, core), mp: 4 (over z).
Axes of the slice: x: 2, y: 2, z: 4, core: 2. Of those that a mesh axis runs over, the one named last changes fastest.
Arguments:
- queries: bfloat16 [2048, 4096], P('dp', 'mp'), may hold values from -6 to 6
- enc_rows: bfloat16 [1024, 4096], P('dp', 'mp'), may hold values from -6 to 6
- key_weight: bfloat16 [4096, 4096], P(None, 'mp'), may hold values from -0.09375 to 0.09375
- value_weight: bfloat16 [4096, 4096], P(None, 'mp'), may hold values from -0.09375 to 0.09375
- enc_len: int32 [8, 8], P('dp'), may hold values from 1 to 64, 128 in all within a row
- dec_len: int32 [8, 8], P('dp'), may hold values from 1 to 128, 256 in all within a row
- route: int32 [8, 8], P('dp'), may hold values from 0 to 7, each once within a row
- out_grad: bfloat16 [2048, 4096], P('dp', 'mp'), may hold values from -6 to 6
Outputs:
- attended: bfloat16 [2048, 4096], P('dp', 'mp')
- query_grad: bfloat16 [2048, 4096], P('dp', 'mp')
- enc_grad: bfloat16 [1024, 4096], P('dp', 'mp')
- key_weight_grad: float32 [4096, 4096], P('dp', 'mp')
- value_weight_grad: float32 [4096, 4096], P('dp', 'mp')
The draws below stay inside these ranges and needn't reach their ends.
Inputs may be any that keep to these rules, and one draw needn't show every extreme that they name: Every row of enc_len sums to 128, and its largest entry is exactly 64. Every row of dec_len sums to 256, and its largest entry is exactly 128. Every row of route is a permutation of the data shards, so each decoder shard receives exactly one example from each shard.
All inputs are finite; a program needn't handle non-finite values.
Results may differ from the reference program's by a relative error of at most 0.013.
Values may be sent and summed in bfloat16 or wider, within the bound.
No kernel may reach another device: no remote copies, remote signals or barrier semaphores. Data moves between devices by JAX's collectives and lax.ppermute only.
A program may use at most 128 MiB of HBM per device.

```python
import math
import jax
import jax.numpy as jnp
import numpy as np
from jax import lax

D = 4096
HEADS = 16
HD = 256
ENC_DEV = 128
DEC_DEV = 256
ENC_MOST = 64
DEC_MOST = 128
ENC_TOTAL = 1024
DEC_TOTAL = 2048
N_DP = 8


def draw_queries(key, part):
    key = jax.random.fold_in(key, 11)
    shape = (DEC_TOTAL, HEADS * HD)
    draws = jnp.clip(jax.random.normal(key, shape, jnp.float32), -6.0, 6.0)
    return draws.astype(jnp.bfloat16)


def with_spikes(values, rng, source, target, parts, factor):
    owner, partner = [(jnp.arange(values.shape[dim]) // (values.shape[dim] // parts)).reshape([-1 if axis == dim else 1 for axis in range(values.ndim)]) for dim in (source, target)]
    chosen = jax.random.permutation(rng, parts)[partner]
    strong = (owner == chosen) | (owner == (partner + parts // 2) % parts)
    return jnp.where(strong, factor * values, values)


def steps_of(own_key, dims, cuts, smallest, largest):
    factor_of = 1.0
    for axis_at, shards_of in cuts:
        steps = jax.random.uniform(jax.random.fold_in(jax.random.fold_in(own_key, 6), axis_at), (shards_of,), jnp.float32, smallest / len(cuts), largest / len(cuts))
        factor_of = factor_of * jnp.repeat(jnp.exp(steps), dims[axis_at] // shards_of).reshape((-1,) + (1,) * (len(dims) - 1 - axis_at))
    return factor_of


def split_up(count, total, bound, lean):
    portions = [(1 << 20) // math.isqrt(rank ** lean) + 1 for rank in range(2, count + 1)]
    surplus, counts = total - bound - (count - 1), [1] * (count - 1)
    while surplus > 0:
        free = [i for i in range(count - 1) if counts[i] < bound]
        whole, left = sum([portions[i] for i in free]), surplus
        for i in free:
            more = min(bound - counts[i], max(1, left * portions[i] // whole), surplus)
            counts[i] = counts[i] + more
            surplus = surplus - more
    return np.array([bound] + counts)


def uneven(rng, count, total, bound, skew):
    if count == 2:
        one = jax.random.randint(rng, (), max(1, total - bound), min(bound, total - 1) + 1)
        return jnp.stack([one, total - one])
    tallies = jnp.asarray(split_up(count, total, bound, skew), jnp.int32)
    pairs = (count - 1) // 2
    giver, sink = tallies[1:1 + 2 * pairs:2], tallies[2:2 + 2 * pairs:2]
    slack = jnp.minimum(giver - 1, bound - sink)
    moved = jax.random.randint(jax.random.fold_in(rng, 1), (pairs,), 0, 1 << 20) % (slack + 1)
    tallies = tallies.at[1:1 + 2 * pairs:2].set(giver - moved).at[2:2 + 2 * pairs:2].set(sink + moved)
    return tallies[jax.random.permutation(jax.random.fold_in(rng, 2), count)]


def centred(key, dims, spread, reach, cuts=(), kind=jnp.bfloat16):
    result = jax.random.normal(key, dims, jnp.float32) * spread
    if len(cuts) > 0:
        result = steps_of(key, dims, cuts, -0.22, 0.18) * result
    return jnp.clip(result, min=-reach, max=reach).astype(kind)


def heavy_noise(own_key, extent, spread, limit, split, heavy, kind=jnp.bfloat16):
    drawn = spread * jax.random.normal(own_key, extent, jnp.float32)
    if split:
        drawn = drawn * steps_of(own_key, extent, split, -0.22, 0.18)
    return jnp.clip(with_spikes(drawn, jax.random.fold_in(own_key, 3), *heavy), -limit, limit).astype(kind)


def setup_inputs(seed: int = 0) -> dict:
    streams_of = jax.random.split(jax.random.key(seed), 9)
    queries = draw_queries(jax.random.fold_in(streams_of[8], 71), 0)
    enc_rows = heavy_noise(streams_of[1], (ENC_TOTAL, D), 1.0, 6.0, ((0, 8), (1, 4)), (0, 1, 8, 2.0))
    key_weight = centred(streams_of[2], (D, HEADS * HD), D ** -0.5, 0.09375, ((1, 4),))
    value_weight = centred(streams_of[3], (D, HEADS * HD), D ** -0.5, 0.09375, ((1, 4),))
    enc_len = jax.vmap(lambda own: uneven(own, N_DP, ENC_DEV, ENC_MOST, 2))(jax.random.split(streams_of[4], N_DP)).reshape((N_DP, N_DP)).astype(jnp.int32)
    dec_len = jax.vmap(lambda own: uneven(own, N_DP, DEC_DEV, DEC_MOST, 2))(jax.random.split(streams_of[5], N_DP)).reshape((N_DP, N_DP)).astype(jnp.int32)
    route = jax.vmap(lambda own: jax.random.permutation(own, N_DP))(jax.random.split(streams_of[6], N_DP)).reshape((N_DP, N_DP)).astype(jnp.int32)
    out_grad = centred(streams_of[7], (DEC_TOTAL, HEADS * HD), 1.0, 6.0, ((0, 8), (1, 4)))
    return {"queries": queries, "enc_rows": enc_rows, "key_weight": key_weight, "value_weight": value_weight, "enc_len": enc_len, "dec_len": dec_len, "route": route, "out_grad": out_grad}


def attend(q_rows, g_rows, key_buf, val_buf, key_live, dec_lens):
    rows = q_rows.shape[0]
    keys_n = key_buf.shape[0]
    heads = q_rows.shape[1] // HD
    scale = HD ** -0.5
    query_h = q_rows.reshape(rows, heads, HD).astype(jnp.float32)
    grad_h = g_rows.reshape(rows, heads, HD).astype(jnp.float32)
    key_h = key_buf.reshape(keys_n, heads, HD).astype(jnp.float32)
    val_h = val_buf.reshape(keys_n, heads, HD).astype(jnp.float32)
    dec_ends = jnp.cumsum(dec_lens, dtype=jnp.int32)
    dec_pos = jnp.arange(rows, dtype=jnp.int32)
    dec_source = jnp.sum((dec_ends[None, :] <= dec_pos[:, None]).astype(jnp.int32), axis=1, dtype=jnp.int32)
    key_source = jnp.arange(keys_n, dtype=jnp.int32) // ENC_MOST
    allowed = (dec_source[:, None] == key_source[None, :]) & key_live[None, :]
    scores = jnp.einsum("qhd,khd->hqk", query_h, key_h) * scale
    scores = jnp.where(allowed[None], scores, -jnp.inf)
    top = jnp.max(scores, axis=-1, keepdims=True)
    expo = jnp.exp(scores - top)
    probs = expo / jnp.sum(expo, axis=-1, keepdims=True)
    weights = probs.astype(jnp.bfloat16)
    attended = jnp.einsum("hqk,khd->qhd", weights.astype(jnp.float32), val_h).astype(jnp.bfloat16)
    dweights = jnp.einsum("qhd,khd->hqk", grad_h, val_h)
    delta = jnp.sum(probs * dweights, axis=-1, keepdims=True)
    dscores = (probs * (dweights - delta) * scale).astype(jnp.bfloat16).astype(jnp.float32)
    query_grad = jnp.einsum("hqk,khd->qhd", dscores, key_h).astype(jnp.bfloat16)
    key_grad = jnp.einsum("hqk,qhd->khd", dscores, query_h).astype(jnp.bfloat16)
    value_grad = jnp.einsum("hqk,qhd->khd", weights.astype(jnp.float32), grad_h).astype(jnp.bfloat16)
    width = heads * HD
    return (attended.reshape(rows, width), query_grad.reshape(rows, width),
            key_grad.reshape(keys_n, width), value_grad.reshape(keys_n, width))


def reference(queries, enc_rows, key_weight, value_weight, enc_len, dec_len, route, out_grad):
    width = HEADS * HD
    keys = jnp.dot(enc_rows, key_weight, preferred_element_type=jnp.float32).astype(jnp.bfloat16)
    values = jnp.dot(enc_rows, value_weight, preferred_element_type=jnp.float32).astype(jnp.bfloat16)
    starts = jnp.cumsum(enc_len, axis=1, dtype=jnp.int32) - enc_len
    shards = jnp.arange(N_DP, dtype=jnp.int32)
    pick = route[:, :, None] == shards[None, None, :]
    start_st = jnp.sum(jnp.where(pick, starts[:, :, None], 0), axis=1, dtype=jnp.int32)
    len_st = jnp.sum(jnp.where(pick, enc_len[:, :, None], 0), axis=1, dtype=jnp.int32)
    offsets = jnp.arange(ENC_MOST, dtype=jnp.int32)
    live = offsets[None, None, :] < len_st.T[:, :, None]
    index = shards[None, :, None] * ENC_DEV + start_st.T[:, :, None] + offsets[None, None, :]
    index = jnp.where(live, index, 0).astype(jnp.int32).reshape(N_DP, N_DP * ENC_MOST)
    live = live.reshape(N_DP, N_DP * ENC_MOST)

    def one_shard(items):
        rows_at, live_at, q_rows, g_rows, lens = items
        key_buf = jnp.where(live_at[:, None], keys[rows_at], jnp.zeros((), jnp.bfloat16))
        val_buf = jnp.where(live_at[:, None], values[rows_at], jnp.zeros((), jnp.bfloat16))
        return attend(q_rows, g_rows, key_buf, val_buf, live_at, lens)

    attended, query_grad, key_slots, value_slots = lax.map(
        one_shard, (index, live, queries.reshape(N_DP, DEC_DEV, width),
                    out_grad.reshape(N_DP, DEC_DEV, width), dec_len))
    flat_index = index.reshape(-1)
    flat_live = live.reshape(-1, 1)
    key_grad = jnp.zeros((ENC_TOTAL, width), jnp.float32).at[flat_index].add(
        jnp.where(flat_live, key_slots.reshape(-1, width).astype(jnp.float32), 0.0)).astype(jnp.bfloat16)
    value_grad = jnp.zeros((ENC_TOTAL, width), jnp.float32).at[flat_index].add(
        jnp.where(flat_live, value_slots.reshape(-1, width).astype(jnp.float32), 0.0)).astype(jnp.bfloat16)
    contract_cols = (((1,), (1,)), ((), ()))
    enc_grad = (lax.dot_general(key_grad, key_weight, contract_cols, preferred_element_type=jnp.float32)
                + lax.dot_general(value_grad, value_weight, contract_cols, preferred_element_type=jnp.float32)).astype(jnp.bfloat16)
    contract_rows = (((0,), (0,)), ((), ()))
    key_weight_grad = lax.dot_general(enc_rows, key_grad, contract_rows, preferred_element_type=jnp.float32)
    value_weight_grad = lax.dot_general(enc_rows, value_grad, contract_rows, preferred_element_type=jnp.float32)
    return (attended.reshape(DEC_TOTAL, width), query_grad.reshape(DEC_TOTAL, width),
            enc_grad, key_weight_grad, value_weight_grad)
```

```python
import functools

import jax
import jax.numpy as jnp
from jax import lax
from jax.experimental import pallas as pl
from jax.experimental.pallas import tpu as pltpu
from jax.sharding import PartitionSpec as P

HD = 256
NT = (((1,), (1,)), ((), ()))
NN = (((1,), (0,)), ((), ()))
TN = (((0,), (0,)), ((), ()))


def mm(a, b, dims):
    return lax.dot_general(a, b, dims, preferred_element_type=jnp.float32)


def attend_kernel(enc_dev, table, dec_len, q_ref, g_ref, k_ref, v_ref, att_ref, qg_ref, kg_ref, vg_ref, open_ref):
    rows = q_ref.shape[0]
    keys_n = k_ref.shape[0]
    shards = dec_len.shape[1]
    scale = HD ** (-0.5)

    @pl.when(pl.program_id(0) == 0)
    def _():
        row = lax.broadcasted_iota(jnp.int32, (rows, 128), 0)
        low = jnp.zeros((rows, 128), jnp.int32)
        high = jnp.zeros((rows, 128), jnp.int32)
        begin = jnp.int32(0)
        for s in range(shards):
            low = jnp.where(row >= begin, table[0, s], low)
            high = jnp.where(row >= begin, table[1, s], high)
            begin = begin + dec_len[0, s]
        for c in range(0, keys_n, 128):
            col = lax.broadcasted_iota(jnp.int32, (rows, 128), 1) + c
            inside = (col >= low) & (col < high)
            open_ref[:, c : c + 128] = jnp.where(inside, 0.0, -jnp.inf)

    q = q_ref[...]
    g = g_ref[...]
    k = k_ref[...]
    v = v_ref[...]
    scores = mm(q, k, NT) * scale + open_ref[...]
    top = jnp.max(scores, axis=1, keepdims=True)
    expo = jnp.exp(scores - top)
    probs = expo * (1.0 / jnp.sum(expo, axis=1, keepdims=True))
    weights = probs.astype(jnp.bfloat16)
    att_ref[...] = mm(weights, v, NN).astype(jnp.bfloat16)
    vg_ref[...] = mm(weights, g, TN).astype(jnp.bfloat16)
    dweights = mm(g, v, NT)
    delta = jnp.sum(probs * dweights, axis=1, keepdims=True)
    dscores = (probs * (dweights - delta) * scale).astype(jnp.bfloat16)
    qg_ref[...] = mm(dscores, k, NN).astype(jnp.bfloat16)
    kg_ref[...] = mm(dscores, q, TN).astype(jnp.bfloat16)


def attend(queries, out_grad, keys, values, table, dec_len, enc_dev):
    rows, width = queries.shape
    keys_n = keys.shape[0]
    heads = width // HD
    row_spec = pl.BlockSpec((rows, HD), lambda h, *_: (0, h))
    key_spec = pl.BlockSpec((keys_n, HD), lambda h, *_: (0, h))
    row_out = jax.ShapeDtypeStruct((rows, width), jnp.bfloat16)
    key_out = jax.ShapeDtypeStruct((keys_n, width), jnp.bfloat16)
    return pl.pallas_call(
        functools.partial(attend_kernel, enc_dev),
        grid_spec=pltpu.PrefetchScalarGridSpec(
            num_scalar_prefetch=2,
            grid=(heads,),
            in_specs=[row_spec, row_spec, key_spec, key_spec],
            out_specs=[row_spec, row_spec, key_spec, key_spec],
            scratch_shapes=[pltpu.VMEM((rows, keys_n), jnp.float32)],
        ),
        out_shape=[row_out, row_out, key_out, key_out],
        compiler_params=pltpu.CompilerParams(vmem_limit_bytes=56 * 2**20),
        cost_estimate=pl.CostEstimate(
            flops=12 * rows * keys_n * width,
            bytes_accessed=2 * (4 * rows * width + 4 * keys_n * width),
            transcendentals=rows * keys_n * heads,
        ),
    )(table, dec_len, queries, out_grad, keys, values)


def body(queries, enc_rows, key_weight, value_weight, enc_len, dec_len, route, out_grad):
    shards = lax.axis_size("dp")
    enc_dev = enc_rows.shape[0]
    me = lax.axis_index("dp")
    lens = enc_len[0]
    targets = route[0]
    order = jnp.arange(shards, dtype=jnp.int32)
    before = order[None, :] < order[:, None]
    starts = jnp.sum(jnp.where(before, lens[None, :], 0), axis=1, dtype=jnp.int32)
    pick = targets[:, None] == order[None, :]
    bounds = me * enc_dev + jnp.stack([starts, starts + lens], axis=1)
    to_dest = jnp.sum(jnp.where(pick[:, :, None], bounds[:, None, :], 0), axis=0, dtype=jnp.int32)
    table = lax.all_to_all(to_dest.reshape(shards, 2), "dp", split_axis=0, concat_axis=0, tiled=True).T

    full = lax.all_gather(enc_rows, "mp", axis=1, tiled=True)
    own_keys = mm(full, key_weight, NN).astype(jnp.bfloat16)
    keys = lax.all_gather(own_keys, "dp", axis=0, tiled=True)
    own_values = mm(full, value_weight, NN).astype(jnp.bfloat16)
    values = lax.all_gather(own_values, "dp", axis=0, tiled=True)
    columns = lax.all_to_all(full, "dp", split_axis=1, concat_axis=0, tiled=True)

    attended, query_grad, key_part, value_part = attend(
        queries, out_grad, keys, values, table, dec_len, enc_dev
    )
    own_vg = lax.psum_scatter(value_part, "dp", scatter_dimension=0, tiled=True)
    own_kg = lax.psum_scatter(key_part, "dp", scatter_dimension=0, tiled=True)
    value_grad = lax.all_gather(own_vg, "dp", axis=0, tiled=True)
    key_grad = lax.all_gather(own_kg, "dp", axis=0, tiled=True)
    part = mm(own_kg, key_weight, NT) + mm(own_vg, value_weight, NT)
    enc_grad = lax.psum_scatter(part.astype(jnp.bfloat16), "mp", scatter_dimension=1, tiled=True)
    value_weight_grad = mm(columns, value_grad, TN)
    key_weight_grad = mm(columns, key_grad, TN)
    return (attended, query_grad, enc_grad, key_weight_grad, value_weight_grad)


def solution(mesh):
    in_specs = (
        P("dp", "mp"),
        P("dp", "mp"),
        P(None, "mp"),
        P(None, "mp"),
        P("dp", None),
        P("dp", None),
        P("dp", None),
        P("dp", "mp"),
    )
    out_specs = (P("dp", "mp"), P("dp", "mp"), P("dp", "mp"), P("dp", "mp"), P("dp", "mp"))
    return jax.shard_map(body, mesh=mesh, in_specs=in_specs, out_specs=out_specs, check_vma=False)
```

```python
import functools

import jax
import jax.numpy as jnp
from jax import lax
from jax.experimental import pallas as pl
from jax.experimental.pallas import tpu as pltpu
from jax.sharding import PartitionSpec as P

HD = 256
GROUPS = 2
NT = (((1,), (1,)), ((), ()))
NN = (((1,), (0,)), ((), ()))
TN = (((0,), (0,)), ((), ()))
SMEM = pl.BlockSpec(memory_space=pltpu.SMEM)
BF16 = jnp.bfloat16
F32 = jnp.float32


def mm(a, b, dims):
    return lax.dot_general(a, b, dims, preferred_element_type=F32)


def params(mib):
    return pltpu.CompilerParams(vmem_limit_bytes=mib * 2**20)


def cost(flops, nbytes, exps=0):
    return pl.CostEstimate(flops=flops, bytes_accessed=nbytes, transcendentals=exps)


def whole(shape):
    return pl.BlockSpec(shape, lambda *_: (0,) * len(shape))


def build_select(sel_ref, me, lens, route, slot):
    shards = lens.shape[1]
    packed = sel_ref.shape[1]
    i = lax.broadcasted_iota(jnp.int32, (slot, packed), 0)
    row = lax.broadcasted_iota(jnp.int32, (slot, packed), 1)
    for r in range(shards):
        target = me ^ r
        start, length, total = jnp.int32(0), jnp.int32(0), jnp.int32(0)
        for j in range(shards):
            hit = route[0, j] == target
            start = jnp.where(hit, total, start)
            length = jnp.where(hit, lens[0, j], length)
            total = total + lens[0, j]
        picked = (row == i + start) & (i < length)
        sel_ref[pl.ds(r * slot, slot), :] = jnp.where(picked, 1.0, 0.0).astype(BF16)


def first_kernel(at, enc_ref, kw_ref, vw_ref, out_ref):
    gw = kw_ref.shape[1]
    enc = enc_ref[...]
    out_ref[:, :gw] = mm(enc, kw_ref[...], NN)
    out_ref[:, gw:] = mm(enc, vw_ref[...], NN)


def first_block(at, enc, key_weight, value_weight):
    rows, depth = enc.shape
    width = key_weight.shape[1]
    gw = width // GROUPS
    w_spec = pl.BlockSpec((depth, gw), lambda g, at: (at[1], g))
    return pl.pallas_call(
        first_kernel,
        grid_spec=pltpu.PrefetchScalarGridSpec(
            num_scalar_prefetch=1,
            grid=(GROUPS,),
            in_specs=[whole((rows, depth)), w_spec, w_spec],
            out_specs=pl.BlockSpec((rows, 2 * gw), lambda g, at: (0, g)),
        ),
        out_shape=jax.ShapeDtypeStruct((rows, 2 * width), F32),
        compiler_params=params(24),
        cost_estimate=cost(4 * rows * depth * width, 4 * depth * width),
    )(at, enc, key_weight, value_weight)


def project_kernel(others, slot, at, lens, route, part_ref, kw_ref, vw_ref, *refs):
    encs = refs[:others]
    outs = refs[others:-2]
    acc_ref, sel_ref = refs[-2:]
    step = pl.program_id(0)
    gw = kw_ref.shape[1]

    @pl.when(step == 0)
    def _():
        acc_ref[...] = part_ref[...]
        build_select(sel_ref, at[0], lens, route, slot)

    for n in range(others):

        @pl.when(step == n)
        def _():
            enc = encs[n][...]
            acc_ref[:, :gw] += mm(enc, kw_ref[...], NN)
            acc_ref[:, gw:] += mm(enc, vw_ref[...], NN)

    @pl.when(step == others - 1)
    def _():
        slots = mm(sel_ref[...], acc_ref[...].astype(BF16), NN).astype(BF16)
        for r, out in enumerate(outs):
            out[...] = slots[r * slot : (r + 1) * slot]


def project(g, slot, at, enc_len, route, part, key_weight, value_weight, encs):
    rows, depth = encs[0].shape
    shards = enc_len.shape[1]
    others = len(encs)
    gw = key_weight.shape[1] // GROUPS
    w_spec = pl.BlockSpec((depth, gw), lambda n, at, *_: ((at[1] + others - n) % (others + 1), g))
    return pl.pallas_call(
        functools.partial(project_kernel, others, slot),
        grid_spec=pltpu.PrefetchScalarGridSpec(
            num_scalar_prefetch=3,
            grid=(others,),
            in_specs=[pl.BlockSpec((rows, 2 * gw), lambda *_: (0, g)), w_spec, w_spec]
            + [whole((rows, depth))] * others,
            out_specs=[whole((slot, 2 * gw))] * shards,
            scratch_shapes=[pltpu.VMEM((rows, 2 * gw), F32), pltpu.VMEM((shards * slot, rows), BF16)],
        ),
        out_shape=[jax.ShapeDtypeStruct((slot, 2 * gw), BF16)] * shards,
        compiler_params=params(24),
        cost_estimate=cost(4 * others * rows * depth * gw, 4 * others * depth * gw),
    )(at, enc_len, route, part, key_weight, value_weight, *encs)


def split_kernel(blocks, shards, at, *refs):
    encs, outs, all_ref = refs[:blocks], refs[blocks:-1], refs[-1]
    size = outs[0].shape[1]
    per = encs[0].shape[1] // size
    for n, enc in enumerate(encs):
        for c in range(per):
            all_ref[n * per + c] = enc[:, c * size : (c + 1) * size]
    for r, out in enumerate(outs):
        target = at[0] ^ r
        n = lax.rem(at[1] + blocks - lax.div(target, per), blocks)
        out[...] = all_ref[n * per + lax.rem(target, per)]


def split_columns(at, encs, shards):
    rows, depth = encs[0].shape
    blocks = len(encs)
    size = blocks * depth // shards
    return pl.pallas_call(
        functools.partial(split_kernel, blocks, shards),
        grid_spec=pltpu.PrefetchScalarGridSpec(
            num_scalar_prefetch=1,
            grid=(1,),
            in_specs=[whole((rows, depth))] * blocks,
            out_specs=[whole((rows, size))] * shards,
            scratch_shapes=[pltpu.VMEM((shards, rows, size), BF16)],
        ),
        out_shape=[jax.ShapeDtypeStruct((rows, size), BF16)] * shards,
        compiler_params=params(16),
        cost_estimate=cost(0, 4 * blocks * rows * depth),
    )(at, *encs)


def attend_kernel(shards, slot, at, counts, dec_len, q_ref, g_ref, *refs):
    msgs = refs[:shards]
    refs = refs[-(2 + shards) - 3 :]
    att_ref, qg_ref = refs[:2]
    outs = refs[2 : 2 + shards]
    open_ref, key_ref, grad_ref = refs[2 + shards :]
    rows, gw = q_ref.shape
    keys_n = shards * slot
    scale = HD ** (-0.5)
    row = lax.broadcasted_iota(jnp.int32, (rows, 128), 0)
    low = jnp.zeros((rows, 128), jnp.int32)
    high = jnp.zeros((rows, 128), jnp.int32)
    begin = jnp.int32(0)
    for s in range(shards):
        place = (at[0] ^ s) * slot
        low = jnp.where(row >= begin, place, low)
        high = jnp.where(row >= begin, place + counts[s, 0], high)
        begin = begin + dec_len[0, s]
    for c in range(0, keys_n, 128):
        col = lax.broadcasted_iota(jnp.int32, (rows, 128), 1) + c
        open_ref[:, c : c + 128] = jnp.where((col >= low) & (col < high), 0.0, -jnp.inf)
    for r, msg in enumerate(msgs):
        key_ref[r * slot : (r + 1) * slot, :] = msg[...]
    for h in range(gw // HD):
        mine = slice(h * HD, (h + 1) * HD)
        theirs = slice(gw + h * HD, gw + (h + 1) * HD)
        q, g, k, v = q_ref[:, mine], g_ref[:, mine], key_ref[:, mine], key_ref[:, theirs]
        scores = mm(q, k, NT) * scale + open_ref[...]
        top = jnp.max(scores, axis=1, keepdims=True)
        expo = jnp.exp(scores - top)
        probs = expo * (1.0 / jnp.sum(expo, axis=1, keepdims=True))
        weights = probs.astype(BF16)
        att_ref[:, mine] = mm(weights, v, NN).astype(BF16)
        grad_ref[:, theirs] = mm(weights, g, TN).astype(BF16)
        dweights = mm(g, v, NT)
        delta = jnp.sum(probs * dweights, axis=1, keepdims=True)
        dscores = (probs * (dweights - delta) * scale).astype(BF16)
        qg_ref[:, mine] = mm(dscores, k, NN).astype(BF16)
        grad_ref[:, mine] = mm(dscores, q, TN).astype(BF16)
    for r, out in enumerate(outs):
        out[...] = grad_ref[r * slot : (r + 1) * slot, :]


def attend(g, slot, at, counts, dec_len, queries, out_grad, msgs, before):
    rows, width = queries.shape
    gw = width // GROUPS
    shards = len(msgs)
    keys_n = shards * slot
    row_spec = pl.BlockSpec((rows, gw), lambda *_: (0, g))
    row_out = jax.ShapeDtypeStruct((rows, width), BF16)
    return pl.pallas_call(
        functools.partial(attend_kernel, shards, slot),
        grid_spec=pltpu.PrefetchScalarGridSpec(
            num_scalar_prefetch=3,
            grid=(1,),
            in_specs=[row_spec] * 2
            + [whole((slot, 2 * gw))] * shards
            + [pl.BlockSpec(memory_space=pl.ANY)] * len(before),
            out_specs=[row_spec] * 2 + [whole((slot, 2 * gw))] * shards,
            scratch_shapes=[
                pltpu.VMEM((rows, keys_n), F32),
                pltpu.VMEM((keys_n, 2 * gw), BF16),
                pltpu.VMEM((keys_n, 2 * gw), BF16),
            ],
        ),
        out_shape=[row_out] * 2 + [jax.ShapeDtypeStruct((slot, 2 * gw), BF16)] * shards,
        input_output_aliases={5 + shards + n: n for n in range(len(before))},
        compiler_params=params(32),
        cost_estimate=cost(12 * rows * keys_n * gw, 8 * (rows + keys_n) * gw, rows * keys_n * (gw // HD)),
    )(at, counts, dec_len, queries, out_grad, *msgs, *before)


def unpack_kernel(shards, slot, at, lens, route, *refs):
    msgs, out_ref, sel_ref, all_ref = refs[:shards], refs[shards], refs[-2], refs[-1]
    build_select(sel_ref, at[0], lens, route, slot)
    for r, msg in enumerate(msgs):
        all_ref[r * slot : (r + 1) * slot, :] = msg[...]
    out_ref[...] = mm(sel_ref[...], all_ref[...], TN).astype(BF16)


def unpack(slot, at, enc_len, route, msgs):
    shards = len(msgs)
    rows = shards * slot // 4
    cols = msgs[0].shape[1]
    return pl.pallas_call(
        functools.partial(unpack_kernel, shards, slot),
        grid_spec=pltpu.PrefetchScalarGridSpec(
            num_scalar_prefetch=3,
            grid=(1,),
            in_specs=[whole((slot, cols))] * shards,
            out_specs=whole((rows, cols)),
            scratch_shapes=[pltpu.VMEM((shards * slot, rows), BF16), pltpu.VMEM((shards * slot, cols), BF16)],
        ),
        out_shape=jax.ShapeDtypeStruct((rows, cols), BF16),
        compiler_params=params(16),
        cost_estimate=cost(2 * shards * slot * rows * cols, 2 * shards * slot * cols),
    )(at, enc_len, route, *msgs)


def back_kernel(chunks, final, at, grad_ref, kw_ref, vw_ref, *refs):
    gw = kw_ref.shape[1]
    step = pl.program_id(0)
    total = mm(grad_ref[:, :gw], kw_ref[...], NT) + mm(grad_ref[:, gw:], vw_ref[...], NT)
    if not final:
        refs[0][0] = total
        return
    total = (total + refs[0][0]).astype(BF16)
    for n, out in enumerate(refs[1:]):

        @pl.when(step == n)
        def _():
            out[...] = total


def project_back(g, chunks, at, grads, key_weight, value_weight, part):
    rows, cols = grads.shape
    gw = cols // 2
    depth = key_weight.shape[0] // chunks
    final = part is not None
    w_spec = pl.BlockSpec((depth, gw), lambda n, at: ((at[1] + n) % chunks, g))
    part_spec = pl.BlockSpec((1, rows, depth), lambda n, at: (n, 0, 0))
    return pl.pallas_call(
        functools.partial(back_kernel, chunks, final),
        grid_spec=pltpu.PrefetchScalarGridSpec(
            num_scalar_prefetch=1,
            grid=(chunks,),
            in_specs=[whole((rows, cols)), w_spec, w_spec] + [part_spec] * final,
            out_specs=[whole((rows, depth))] * chunks if final else part_spec,
        ),
        out_shape=[jax.ShapeDtypeStruct((rows, depth), BF16)] * chunks
        if final
        else jax.ShapeDtypeStruct((chunks, rows, depth), F32),
        compiler_params=params(24),
        cost_estimate=cost(2 * rows * cols * depth * chunks, 2 * cols * depth * chunks),
    )(at, grads, key_weight, value_weight, *([part] if final else []))


def weight_grad_kernel(shards, *refs):
    cols, grads = refs[:shards], refs[shards : 2 * shards]
    kout, vout, col_ref, grad_ref = refs[-4:]
    gw = kout.shape[1]
    rows = cols[0].shape[0]
    for r in range(shards):
        col_ref[r * rows : (r + 1) * rows, :] = cols[r][...]
        grad_ref[r * rows : (r + 1) * rows, :] = grads[r][...]
    kout[...] = mm(col_ref[...], grad_ref[:, :gw], TN)
    vout[...] = mm(col_ref[...], grad_ref[:, gw:], TN)


def weight_grads(g, cols, grads, width, before):
    shards = len(cols)
    rows, size = cols[0].shape
    gw = width // GROUPS
    out_spec = pl.BlockSpec((size, gw), lambda *_: (0, g))
    return pl.pallas_call(
        functools.partial(weight_grad_kernel, shards),
        grid=(1,),
        in_specs=[whole((rows, size))] * shards
        + [whole((rows, 2 * gw))] * shards
        + [pl.BlockSpec(memory_space=pl.ANY)] * len(before),
        out_specs=[out_spec] * 2,
        scratch_shapes=[pltpu.VMEM((shards * rows, size), BF16), pltpu.VMEM((shards * rows, 2 * gw), BF16)],
        out_shape=[jax.ShapeDtypeStruct((size, width), F32)] * 2,
        input_output_aliases={2 * shards + n: n for n in range(len(before))},
        compiler_params=params(40),
        cost_estimate=cost(4 * shards * rows * size * gw, 2 * shards * rows * (size + 2 * gw) + 8 * size * gw),
    )(*cols, *grads, *before)


def body(queries, enc_rows, key_weight, value_weight, enc_len, dec_len, route, out_grad):
    shards = lax.axis_size("dp")
    peers = lax.axis_size("mp")
    enc_dev = enc_rows.shape[0]
    slot = 4 * enc_dev // shards
    width = key_weight.shape[1]
    at = jnp.stack([lax.axis_index("dp"), lax.axis_index("mp")]).astype(jnp.int32)

    def flip(x, r):
        return lax.ppermute(x, "dp", [(i, i ^ r) for i in range(shards)])

    def shift(x, r):
        return lax.ppermute(x, "mp", [(i, (i + r) % peers) for i in range(peers)])

    encs = [shift(enc_rows, r) for r in range(1, peers)]
    order = jnp.arange(shards, dtype=jnp.int32)
    pick = route[0][:, None] == order[None, :]
    sends = jnp.sum(jnp.where(pick, enc_len[0][:, None], 0), axis=0, dtype=jnp.int32)
    counts = lax.all_to_all(sends.reshape(shards, 1), "dp", split_axis=0, concat_axis=0, tiled=True)

    part = first_block(at, enc_rows, key_weight, value_weight)
    back_part = None
    rows_out = []
    weight_out = []
    held = []
    for g in range(GROUPS):
        slots = project(g, slot, at, enc_len, route, part, key_weight, value_weight, encs)
        held.append([slots[0]] + [flip(slots[r], r) for r in range(1, shards)])
    cols = split_columns(at, [enc_rows] + encs, shards)
    cols = [cols[0]] + [flip(cols[r], r) for r in range(1, shards)]
    for g in range(GROUPS):
        out = attend(g, slot, at, counts, dec_len, queries, out_grad, held[g], rows_out)
        rows_out = out[:2]
        msgs = [out[2]] + [flip(out[2 + r], r) for r in range(1, shards)]
        own = unpack(slot, at, enc_len, route, msgs)
        back_part = project_back(g, peers, at, own, key_weight, value_weight, back_part)
        grads = [own] + [None] * (shards - 1)
        for r in range(2, shards, 2):
            grads[r] = flip(own, r)
        for r in range(1, shards, 2):
            grads[r] = flip(grads[r - 1], 1)
        weight_out = weight_grads(g, cols, grads, width, weight_out)
    total = back_part[0].astype(F32)
    for r in range(1, peers):
        total = total + shift(back_part[r], r).astype(F32)
    return (rows_out[0], rows_out[1], total.astype(BF16), weight_out[0], weight_out[1])


def solution(mesh):
    in_specs = (
        P("dp", "mp"),
        P("dp", "mp"),
        P(None, "mp"),
        P(None, "mp"),
        P("dp", None),
        P("dp", None),
        P("dp", None),
        P("dp", "mp"),
    )
    out_specs = (P("dp", "mp"), P("dp", "mp"), P("dp", "mp"), P("dp", "mp"), P("dp", "mp"))
    return jax.shard_map(body, mesh=mesh, in_specs=in_specs, out_specs=out_specs, check_vma=False)
```

```python
import functools

import jax
import jax.numpy as jnp
from jax import lax
from jax.experimental import pallas as pl
from jax.experimental.pallas import tpu as pltpu
from jax.sharding import PartitionSpec as P

HD = 256
TILE = 256
NT = (((1,), (1,)), ((), ()))
NN = (((1,), (0,)), ((), ()))
TN = (((0,), (0,)), ((), ()))
SMEM = pl.BlockSpec(memory_space=pltpu.SMEM)
BF16 = jnp.bfloat16
F32 = jnp.float32


def mm(a, b, dims):
    return lax.dot_general(a, b, dims, preferred_element_type=F32)


def params(mib=60):
    return pltpu.CompilerParams(vmem_limit_bytes=mib * 2**20)


def cost(flops, nbytes, exps=0):
    return pl.CostEstimate(flops=flops, bytes_accessed=nbytes, transcendentals=exps)


def whole(shape):
    return pl.BlockSpec(shape, lambda *_: (0,) * len(shape))


def pair_rows(ref, core, own, partner):
    rows = own.shape[0]
    ref[pl.ds(pl.multiple_of(core * rows, rows), rows), :] = own
    ref[pl.ds(pl.multiple_of((1 - core) * rows, rows), rows), :] = partner


def project_kernel(first, blocks, cuts, final, at, kw_ref, vw_ref, *refs):
    owns, partners = refs[:blocks], refs[blocks : 2 * blocks]
    enc_ref, acc_ref, w_ref, sems = refs[-4:]
    _, steps, tile, gw = w_ref.shape
    peers = kw_ref.shape[0] // (cuts * tile)
    core = at[0] & 1
    copies = []
    for n in range(steps):
        block = lax.rem(at[1] + 2 * peers - first - n // cuts, peers)
        rows = pl.ds(pl.multiple_of((block * cuts + n % cuts) * tile, tile), tile)
        cols = pl.ds(pl.multiple_of(core * gw, gw), gw)
        for m, ref in enumerate((kw_ref, vw_ref)):
            copies.append(pltpu.make_async_copy(ref.at[rows, cols], w_ref.at[m, n], sems.at[m, n]))
            copies[-1].start()
    for n in range(steps):
        place = slice(n % cuts * tile, (n % cuts + 1) * tile)
        pair_rows(enc_ref.at[n], core, owns[n // cuts][:, place], partners[n // cuts][:, place])
    acc_ref[...] = refs[2 * blocks][...] if final else jnp.zeros_like(acc_ref)
    for n in range(steps):
        copies[2 * n].wait()
        copies[2 * n + 1].wait()
        acc_ref[:, :gw] += mm(enc_ref[n], w_ref[0, n], NN)
        acc_ref[:, gw:] += mm(enc_ref[n], w_ref[1, n], NN)
    if final:
        refs[-6][...] = acc_ref[:, :gw].astype(BF16)
        refs[-5][...] = acc_ref[:, gw:].astype(BF16)
    else:
        refs[-5][...] = acc_ref[...]


def project(first, at, key_weight, value_weight, owns, partners, sums=None):
    rows, depth = owns[0].shape
    gw = key_weight.shape[1] // 2
    blocks = len(owns)
    final = sums is not None
    cuts = 2
    tile = depth // cuts
    out_shape = (2 * rows, 2 * gw)
    half = (2 * rows, gw)
    return pl.pallas_call(
        functools.partial(project_kernel, first, blocks, cuts, final),
        grid_spec=pltpu.PrefetchScalarGridSpec(
            num_scalar_prefetch=1,
            grid=(1,),
            in_specs=[pl.BlockSpec(memory_space=pltpu.HBM)] * 2
            + [whole((rows, depth))] * (2 * blocks)
            + [whole(out_shape)] * final,
            out_specs=[whole(half)] * 2 if final else whole(out_shape),
            scratch_shapes=[
                pltpu.VMEM((blocks * cuts, 2 * rows, tile), BF16),
                pltpu.VMEM(out_shape, F32),
                pltpu.VMEM((2, blocks * cuts, tile, gw), BF16),
                pltpu.SemaphoreType.DMA((2, blocks * cuts)),
            ],
        ),
        out_shape=[jax.ShapeDtypeStruct(half, BF16)] * 2 if final else jax.ShapeDtypeStruct(out_shape, F32),
        compiler_params=params(22),
        cost_estimate=cost(8 * blocks * rows * depth * gw, 4 * blocks * depth * gw),
    )(at, key_weight, value_weight, *owns, *partners, *([sums] if final else []))


def split_kernel(peers, at, *refs):
    owns, partners = refs[:peers], refs[peers : 2 * peers]
    outs, all_ref = refs[2 * peers : -1], refs[-1]
    size = outs[0].shape[1]
    per = owns[0].shape[1] // size
    for r in range(peers):
        for c in range(per):
            place = slice(c * size, (c + 1) * size)
            pair_rows(all_ref.at[r * per + c], at[0] & 1, owns[r][:, place], partners[r][:, place])
    for j, out in enumerate(outs):
        target = at[0] ^ (2 * j)
        r = lax.rem(at[1] + peers - lax.div(target, per), peers)
        out[...] = all_ref[r * per + lax.rem(target, per)]


def split_columns(chips, at, owns, partners):
    rows, depth = owns[0].shape
    peers = len(owns)
    size = peers * depth // (2 * chips)
    return pl.pallas_call(
        functools.partial(split_kernel, peers),
        grid_spec=pltpu.PrefetchScalarGridSpec(
            num_scalar_prefetch=1,
            grid=(1,),
            in_specs=[whole((rows, depth))] * (2 * peers),
            out_specs=[whole((2 * rows, size))] * chips,
            scratch_shapes=[pltpu.VMEM((2 * chips, 2 * rows, size), BF16)],
        ),
        out_shape=[jax.ShapeDtypeStruct((2 * rows, size), BF16)] * chips,
        compiler_params=params(16),
        cost_estimate=cost(0, 8 * peers * rows * depth),
    )(at, *owns, *partners)


def attend_kernel(chips, window, at, table, q_ref, g_ref, pair_ref, *refs):
    keys, values = refs[:chips], refs[chips : 2 * chips]
    att_ref, qg_ref, back_ref = refs[2 * chips : 2 * chips + 3]
    outs = refs[2 * chips + 3 : -3]
    outs = (outs[:chips], outs[chips:])
    open_ref, key_ref, grad_ref = refs[-3:]
    rows, gw = q_ref.shape
    shards = 2 * chips
    packed = keys[0].shape[0] // 2
    keys_n = shards * window
    scale = HD ** (-0.5)
    for out in outs[0] + outs[1]:
        out[...] = jnp.zeros_like(out)
    for d in range(2):
        row = lax.broadcasted_iota(jnp.int32, (rows, 128), 0)
        low = jnp.zeros((rows, 128), jnp.int32)
        high = jnp.zeros((rows, 128), jnp.int32)
        for s in range(shards):
            place = (s ^ (at[0] & -2)) * window
            low = jnp.where(row >= table[3, d, s], place + table[1, d, s], low)
            high = jnp.where(row >= table[3, d, s], place + table[2, d, s], high)
        for c in range(0, keys_n, 128):
            col = lax.broadcasted_iota(jnp.int32, (rows, 128), 1) + c
            open_ref[d, :, c : c + 128] = jnp.where((col >= low) & (col < high), 0.0, -jnp.inf)
        bases = []
        for u in range(shards):
            bases.append(pl.multiple_of(u % 2 * packed + table[0, d, u ^ (at[0] & -2)], 16))
            key_ref[d, u * window : (u + 1) * window, :gw] = keys[u // 2][pl.ds(bases[u], window), :]
            key_ref[d, u * window : (u + 1) * window, gw:] = values[u // 2][pl.ds(bases[u], window), :]
        for h in range(gw // HD):
            mine = slice(h * HD, (h + 1) * HD)
            theirs = slice(gw + h * HD, gw + (h + 1) * HD)
            q, g = (pair_ref[:, mine], pair_ref[:, theirs]) if d else (q_ref[:, mine], g_ref[:, mine])
            k, v = key_ref[d, :, mine], key_ref[d, :, theirs]
            scores = mm(q, k, NT) * scale + open_ref[d]
            top = jnp.max(scores, axis=1, keepdims=True)
            expo = jnp.exp(scores - top)
            probs = expo * (1.0 / jnp.sum(expo, axis=1, keepdims=True))
            weights = probs.astype(BF16)
            attended = mm(weights, v, NN).astype(BF16)
            grad_ref[d, :, theirs] = mm(weights, g, TN).astype(BF16)
            dweights = mm(g, v, NT)
            delta = jnp.sum(probs * dweights, axis=1, keepdims=True)
            dscores = (probs * (dweights - delta) * scale).astype(BF16)
            query_grad = mm(dscores, k, NN).astype(BF16)
            grad_ref[d, :, mine] = mm(dscores, q, TN).astype(BF16)
            if d:
                back_ref[:, mine], back_ref[:, theirs] = attended, query_grad
            else:
                att_ref[:, mine], qg_ref[:, mine] = attended, query_grad
        for u in range(shards):
            for m in range(2):
                part = grad_ref[d, u * window : (u + 1) * window, m * gw : (m + 1) * gw]
                outs[m][u // 2][pl.ds(bases[u], window), :] += part


def attend(window, at, table, queries, out_grad, pair, keys, values):
    rows, width = queries.shape
    gw = width // 2
    chips = len(keys)
    keys_n = 2 * chips * window
    row_spec = pl.BlockSpec((rows, gw), lambda n, at, *_: (0, at[0] & 1))
    half = jax.ShapeDtypeStruct((rows, gw), BF16)
    both = jax.ShapeDtypeStruct((rows, width), BF16)
    block = keys[0].shape
    return pl.pallas_call(
        functools.partial(attend_kernel, chips, window),
        grid_spec=pltpu.PrefetchScalarGridSpec(
            num_scalar_prefetch=2,
            grid=(1,),
            in_specs=[row_spec] * 2 + [whole((rows, width))] + [whole(keys[0].shape)] * (2 * chips),
            out_specs=[whole((rows, gw))] * 2 + [whole((rows, width))] + [whole(block)] * (2 * chips),
            scratch_shapes=[
                pltpu.VMEM((2, rows, keys_n), F32),
                pltpu.VMEM((2, keys_n, width), BF16),
                pltpu.VMEM((2, keys_n, width), BF16),
            ],
        ),
        out_shape=[half, half, both] + [jax.ShapeDtypeStruct(block, BF16)] * (2 * chips),
        compiler_params=params(20 if keys_n <= 640 else 28),
        cost_estimate=cost(24 * rows * keys_n * gw, 8 * rows * width + 4 * keys_n * width, 4 * rows * keys_n),
    )(at, table, queries, out_grad, pair, *keys, *values)


def back_kernel(r, chunks, at, ko_ref, vo_ref, kp_ref, vp_ref, kw_ref, vw_ref, out_ref, w_ref, turned_ref, sems):
    depth, rows = out_ref.shape
    gw = ko_ref.shape[1]
    tile = min(TILE, depth)
    steps = depth // tile
    first = lax.rem(at[1] + r, chunks) * depth
    copies = []
    for n in range(steps):
        for m, ref in enumerate((kw_ref, vw_ref)):
            place = pl.ds(pl.multiple_of(first + n * tile, tile), tile)
            copies.append(pltpu.make_async_copy(ref.at[place, :], w_ref.at[m, n], sems.at[m, n]))
            copies[-1].start()
    for n, pair in enumerate(((ko_ref, vo_ref), (kp_ref, vp_ref))):
        start = pl.multiple_of(((at[0] & 1) ^ n) * gw, gw)
        for m, ref in enumerate(pair):
            turned_ref[m, pl.ds(start, gw), :] = ref[...].astype(F32).T.astype(BF16)
    for n in range(steps):
        copies[2 * n].wait()
        copies[2 * n + 1].wait()
        total = mm(w_ref[0, n], turned_ref[0], NN) + mm(w_ref[1, n], turned_ref[1], NN)
        out_ref[n * tile : (n + 1) * tile, :] = total.astype(BF16)


def project_back(r, chunks, at, own, other, key_weight, value_weight):
    rows, gw = own[0].shape
    rows = rows // 2
    depth = key_weight.shape[0] // chunks
    tile = min(TILE, depth)
    steps = depth // tile
    row_spec = pl.BlockSpec((rows, gw), lambda n, at: (at[0] & 1, 0))
    return pl.pallas_call(
        functools.partial(back_kernel, r, chunks),
        grid_spec=pltpu.PrefetchScalarGridSpec(
            num_scalar_prefetch=1,
            grid=(1,),
            in_specs=[row_spec] * 4 + [pl.BlockSpec(memory_space=pltpu.HBM)] * 2,
            out_specs=whole((depth, rows)),
            scratch_shapes=[
                pltpu.VMEM((2, steps, tile, 2 * gw), BF16),
                pltpu.VMEM((2, 2 * gw, rows), BF16),
                pltpu.SemaphoreType.DMA((2, steps)),
            ],
        ),
        out_shape=jax.ShapeDtypeStruct((depth, rows), BF16),
        compiler_params=params(16),
        cost_estimate=cost(8 * rows * gw * depth, 8 * gw * depth),
    )(at, *own, *other, key_weight, value_weight)


def weight_grad_kernel(chips, at, col_ref, *refs):
    grads = refs[: 4 * chips]
    outs = refs[4 * chips : -1]
    grad_ref = refs[-1]
    rows = grads[0].shape[0]
    half = pl.program_id(0) // (pl.num_programs(0) // 2)
    for m in range(2):

        @pl.when(half == m)
        def _():
            for n, out in enumerate(outs):
                for j in range(chips):
                    grad_ref[n, j * rows : (j + 1) * rows, :] = grads[(2 * m + n) * chips + j][...]
                out[...] = mm(col_ref[...], grad_ref[n], NN)


def weight_grads(at, cols, owns, others):
    chips = len(owns[0])
    rows, gw = owns[0][0].shape
    width = 2 * gw
    size = cols.shape[0]
    steps = gw // TILE
    own_spec = pl.BlockSpec((rows, TILE), lambda n, at: (0, jnp.minimum(n, steps - 1)))
    other_spec = pl.BlockSpec((rows, TILE), lambda n, at: (0, jnp.maximum(n - steps, 0)))
    out_spec = pl.BlockSpec((size, TILE), lambda n, at: (0, (n // steps ^ (at[0] & 1)) * steps + n % steps))
    return pl.pallas_call(
        functools.partial(weight_grad_kernel, chips),
        grid_spec=pltpu.PrefetchScalarGridSpec(
            num_scalar_prefetch=1,
            grid=(2 * steps,),
            in_specs=[whole(cols.shape)] + [own_spec] * (2 * chips) + [other_spec] * (2 * chips),
            out_specs=[out_spec] * 2,
            scratch_shapes=[pltpu.VMEM((2, chips * rows, TILE), BF16)],
        ),
        out_shape=[jax.ShapeDtypeStruct((size, width), F32)] * 2,
        compiler_params=params(16 if chips <= 4 else 28),
        cost_estimate=cost(4 * chips * rows * size * width, 2 * chips * rows * (size + 2 * width) + 8 * size * width),
    )(at, cols, *owns[0], *owns[1], *others[0], *others[1])


def window_table(dp, enc_len, route, dec_len, window):
    shards = enc_len.shape[1]
    packed_rows = jnp.concatenate([enc_len, route, dec_len], axis=1)
    everyone = lax.all_to_all(
        jnp.broadcast_to(packed_rows, (shards, 3 * shards)), "dp", split_axis=0, concat_axis=0, tiled=True
    )
    lens, targets, decs = everyone[:, :shards], everyone[:, shards : 2 * shards], everyone[:, 2 * shards :]
    order = jnp.arange(shards, dtype=jnp.int32)
    before = (order[None, :] < order[:, None])[None]
    starts = jnp.sum(jnp.where(before, lens[:, None, :], 0), axis=2, dtype=jnp.int32)
    here = dp ^ jnp.arange(2, dtype=jnp.int32)
    hit = targets[None] == here[:, None, None]
    start = jnp.sum(jnp.where(hit, starts[None], 0), axis=2, dtype=jnp.int32)
    length = jnp.sum(jnp.where(hit, lens[None], 0), axis=2, dtype=jnp.int32)
    mine = jnp.sum(jnp.where((order[None] == here[:, None])[:, :, None], decs[None], 0), axis=1, dtype=jnp.int32)
    begin = jnp.sum(jnp.where(before, mine[:, None, :], 0), axis=2, dtype=jnp.int32)
    return start, length, begin


def body(queries, enc_rows, key_weight, value_weight, enc_len, dec_len, route, out_grad):
    shards = lax.axis_size("dp")
    peers = lax.axis_size("mp")
    chips = shards // 2
    packed = enc_rows.shape[0]
    window = 4 * packed // shards + 16
    gw = key_weight.shape[1] // 2
    dp, mp = lax.axis_index("dp"), lax.axis_index("mp")
    core = dp & 1
    at = jnp.stack([dp, mp]).astype(jnp.int32)

    def flip(x, r):
        return lax.ppermute(x, "dp", [(i, i ^ r) for i in range(shards)])

    def shift(x, r):
        return lax.ppermute(x, "mp", [(i, (i + r) % peers) for i in range(peers)])

    low = 1 << ((chips.bit_length() - 1) // 2)
    lows, highs = range(1, low), range(low, chips, low)

    def spread(x, low_first):
        got = {0: x}
        first, second = (lows, highs) if low_first else (highs, lows)
        for a in first:
            got[a] = flip(x, 2 * a)
        for b in second:
            got[b] = flip(x, 2 * b)
        for a in first:
            for b in second:
                got[a + b] = flip(got[a], 2 * b)
        return [got[j] for j in range(chips)]

    def collect(parts, low_first):
        first, second = (lows, highs) if low_first else (highs, lows)
        sums = {}
        for b in [*second, 0]:
            sums[b] = functools.reduce(jnp.add, [parts[b]] + [flip(parts[a + b], 2 * a) for a in first])
        return functools.reduce(jnp.add, [flip(sums[b], 2 * b) for b in second] + [sums[0]])

    partner = flip(enc_rows, 1)
    owns = [enc_rows] + [shift(enc_rows, r) for r in range(1, peers)]
    sums = project(0, at, key_weight, value_weight, [enc_rows], [partner])
    sums, owns = lax.optimization_barrier((sums, owns))
    partners = [partner] + [flip(x, 1) for x in owns[1:]]
    keys, values = project(1, at, key_weight, value_weight, owns[1:], partners[1:], sums)
    keys, values, lens, targets, decs, *theirs = lax.optimization_barrier(
        (keys, values, enc_len, route, dec_len, queries, out_grad)
    )
    keys, values = spread(keys, True), spread(values, False)
    theirs = [lax.dynamic_slice_in_dim(x, (1 - core) * gw, gw, axis=1) for x in theirs]
    pair = flip(jnp.concatenate(theirs, axis=1), 1)
    start, length, begin = window_table(dp, lens, targets, decs, window)
    base = jnp.minimum(start // 16 * 16, packed - window)
    table = jnp.stack([base, start - base, start - base + length, begin])
    cols = split_columns(chips, at, owns, partners)
    keys, values, table, pair, cols = lax.optimization_barrier((keys, values, table, pair, list(cols)))
    cols = [cols[0]] + [flip(cols[j], 2 * j) for j in range(1, chips)]
    attended, query_grad, back, *parts = attend(window, at, table, queries, out_grad, pair, keys, values)
    parts, back, cols = lax.optimization_barrier((parts, back, cols))
    own = [collect(parts[:chips], False), collect(parts[chips:], True)]
    back = flip(back, 1)
    outs = []
    for mine, rest in ((attended, back[:, :gw]), (query_grad, back[:, gw:])):
        outs.append(jnp.where(core == 0, jnp.concatenate([mine, rest], 1), jnp.concatenate([rest, mine], 1)))
    cols = jnp.concatenate([x.T for x in cols], axis=1)
    own, cols, outs = lax.optimization_barrier((own, cols, outs))
    other = [flip(x, 1) for x in own]
    owns = [spread(own[0], True), spread(own[1], False)]
    middle = peers // 2
    order = [middle] + [r for r in range(1, peers) if r != middle] + [0]
    chunks = [project_back(r, peers, at, own, other, key_weight, value_weight) for r in order]
    arrived = [shift(x, r) for x, r in zip(chunks[:-1], order)]
    owns, arrived[0], _, chunk = lax.optimization_barrier((owns, arrived[0], chunks[:-1], chunks[-1]))
    others = [[other[n]] + [flip(x, 1) for x in owns[n][1:]] for n in range(2)]
    weight_out = weight_grads(at, cols, owns, others)
    arrived, weight_out = lax.optimization_barrier((arrived, weight_out))
    total = functools.reduce(jnp.add, [x.astype(F32) for x in [chunk, *arrived]])
    return (*outs, total.T.astype(BF16), *weight_out)


def solution(mesh):
    in_specs = (
        P("dp", "mp"),
        P("dp", "mp"),
        P(None, "mp"),
        P(None, "mp"),
        P("dp", None),
        P("dp", None),
        P("dp", None),
        P("dp", "mp"),
    )
    out_specs = (P("dp", "mp"), P("dp", "mp"), P("dp", "mp"), P("dp", "mp"), P("dp", "mp"))
    return jax.shard_map(body, mesh=mesh, in_specs=in_specs, out_specs=out_specs, check_vma=False)
```

```python
import functools

import jax
import jax.numpy as jnp
from jax import lax
from jax.experimental import pallas as pl
from jax.experimental.pallas import tpu as pltpu
from jax.sharding import PartitionSpec as P

HD = 256
TILE = 256
NT = (((1,), (1,)), ((), ()))
NN = (((1,), (0,)), ((), ()))
TN = (((0,), (0,)), ((), ()))
SMEM = pl.BlockSpec(memory_space=pltpu.SMEM)
BF16 = jnp.bfloat16
F32 = jnp.float32


def mm(a, b, dims):
    return lax.dot_general(a, b, dims, preferred_element_type=F32)


def params(mib=60):
    return pltpu.CompilerParams(vmem_limit_bytes=mib * 2**20)


def cost(flops, nbytes, exps=0):
    return pl.CostEstimate(flops=flops // 1024, bytes_accessed=nbytes // 1024, transcendentals=exps // 1024)


def whole(shape):
    return pl.BlockSpec(shape, lambda *_: (0,) * len(shape))


def pair_rows(ref, core, own, partner):
    rows = own.shape[0]
    ref[pl.ds(pl.multiple_of(core * rows, rows), rows), :] = own
    ref[pl.ds(pl.multiple_of((1 - core) * rows, rows), rows), :] = partner


def project_kernel(first, blocks, cuts, final, at, kw_ref, vw_ref, *refs):
    owns, partners = refs[:blocks], refs[blocks : 2 * blocks]
    enc_ref, acc_ref, w_ref, sems = refs[-4:]
    _, steps, tile, gw = w_ref.shape
    peers = kw_ref.shape[0] // (cuts * tile)
    core = at[0] & 1
    copies = []
    for n in range(steps):
        block = lax.rem(at[1] + 2 * peers - first - n // cuts, peers)
        rows = pl.ds(pl.multiple_of((block * cuts + n % cuts) * tile, tile), tile)
        cols = pl.ds(pl.multiple_of(core * gw, gw), gw)
        for m, ref in enumerate((kw_ref, vw_ref)):
            copies.append(pltpu.make_async_copy(ref.at[rows, cols], w_ref.at[m, n], sems.at[m, n]))
            copies[-1].start()
    for n in range(steps):
        place = slice(n % cuts * tile, (n % cuts + 1) * tile)
        pair_rows(enc_ref.at[n], core, owns[n // cuts][:, place], partners[n // cuts][:, place])
    acc_ref[...] = refs[2 * blocks][...] if final else jnp.zeros_like(acc_ref)
    for n in range(steps):
        copies[2 * n].wait()
        copies[2 * n + 1].wait()
        acc_ref[:, :gw] += mm(enc_ref[n], w_ref[0, n], NN)
        acc_ref[:, gw:] += mm(enc_ref[n], w_ref[1, n], NN)
    if final:
        refs[-6][...] = acc_ref[:, :gw].astype(BF16)
        refs[-5][...] = acc_ref[:, gw:].astype(BF16)
    else:
        refs[-5][...] = acc_ref[...]


def project(first, at, key_weight, value_weight, owns, partners, sums=None):
    rows, depth = owns[0].shape
    gw = key_weight.shape[1] // 2
    blocks = len(owns)
    final = sums is not None
    cuts = 2
    tile = depth // cuts
    out_shape = (2 * rows, 2 * gw)
    half = (2 * rows, gw)
    return pl.pallas_call(
        functools.partial(project_kernel, first, blocks, cuts, final),
        grid_spec=pltpu.PrefetchScalarGridSpec(
            num_scalar_prefetch=1,
            grid=(1,),
            in_specs=[pl.BlockSpec(memory_space=pltpu.HBM)] * 2
            + [whole((rows, depth))] * (2 * blocks)
            + [whole(out_shape)] * final,
            out_specs=[whole(half)] * 2 if final else whole(out_shape),
            scratch_shapes=[
                pltpu.VMEM((blocks * cuts, 2 * rows, tile), BF16),
                pltpu.VMEM(out_shape, F32),
                pltpu.VMEM((2, blocks * cuts, tile, gw), BF16),
                pltpu.SemaphoreType.DMA((2, blocks * cuts)),
            ],
        ),
        out_shape=[jax.ShapeDtypeStruct(half, BF16)] * 2 if final else jax.ShapeDtypeStruct(out_shape, F32),
        compiler_params=params(48),
        cost_estimate=cost(8 * blocks * rows * depth * gw, 4 * blocks * depth * gw),
    )(at, key_weight, value_weight, *owns, *partners, *([sums] if final else []))


def split_kernel(peers, at, *refs):
    owns, partners = refs[:peers], refs[peers : 2 * peers]
    outs, all_ref = refs[2 * peers : -1], refs[-1]
    size = outs[0].shape[0]
    per = owns[0].shape[1] // size
    for r in range(peers):
        for c in range(per):
            place = slice(c * size, (c + 1) * size)
            pair_rows(all_ref.at[r * per + c], at[0] & 1, owns[r][:, place], partners[r][:, place])
    for j, out in enumerate(outs):
        target = at[0] ^ (2 * j)
        r = lax.rem(at[1] + peers - lax.div(target, per), peers)
        out[...] = all_ref[r * per + lax.rem(target, per)].astype(F32).T.astype(BF16)


def split_columns(chips, at, owns, partners):
    rows, depth = owns[0].shape
    peers = len(owns)
    size = peers * depth // (2 * chips)
    return pl.pallas_call(
        functools.partial(split_kernel, peers),
        grid_spec=pltpu.PrefetchScalarGridSpec(
            num_scalar_prefetch=1,
            grid=(1,),
            in_specs=[whole((rows, depth))] * (2 * peers),
            out_specs=[whole((size, 2 * rows))] * chips,
            scratch_shapes=[pltpu.VMEM((2 * chips, 2 * rows, size), BF16)],
        ),
        out_shape=[jax.ShapeDtypeStruct((size, 2 * rows), BF16)] * chips,
        compiler_params=params(16),
        cost_estimate=cost(0, 8 * peers * rows * depth),
    )(at, *owns, *partners)


def attend_kernel(chips, window, at, table, own_ref, pair_ref, *refs):
    keys, values = refs[:chips], refs[chips : 2 * chips]
    att_ref, qg_ref, back_ref = refs[2 * chips : 2 * chips + 3]
    outs = refs[2 * chips + 3 : -3]
    outs = (outs[:chips], outs[chips:])
    open_ref, key_ref, grad_ref = refs[-3:]
    rows, gw = att_ref.shape
    shards = 2 * chips
    packed = keys[0].shape[0] // 2
    keys_n = shards * window
    scale = HD ** (-0.5)
    for out in outs[0] + outs[1]:
        out[...] = jnp.zeros_like(out)
    for d in range(2):
        row = lax.broadcasted_iota(jnp.int32, (rows, 128), 0)
        low = jnp.zeros((rows, 128), jnp.int32)
        high = jnp.zeros((rows, 128), jnp.int32)
        for s in range(shards):
            place = (s ^ (at[0] & -2)) * window
            low = jnp.where(row >= table[3, d, s], place + table[1, d, s], low)
            high = jnp.where(row >= table[3, d, s], place + table[2, d, s], high)
        for c in range(0, keys_n, 128):
            col = lax.broadcasted_iota(jnp.int32, (rows, 128), 1) + c
            open_ref[d, :, c : c + 128] = jnp.where((col >= low) & (col < high), 0.0, -jnp.inf)
        bases = []
        for u in range(shards):
            bases.append(pl.multiple_of(u % 2 * packed + table[0, d, u ^ (at[0] & -2)], 16))
            key_ref[d, u * window : (u + 1) * window, :gw] = keys[u // 2][pl.ds(bases[u], window), :]
            key_ref[d, u * window : (u + 1) * window, gw:] = values[u // 2][pl.ds(bases[u], window), :]
        for h in range(gw // HD):
            mine = slice(h * HD, (h + 1) * HD)
            theirs = slice(gw + h * HD, gw + (h + 1) * HD)
            q, g = ((own_ref, pair_ref)[d][:, place] for place in (mine, theirs))
            k, v = key_ref[d, :, mine], key_ref[d, :, theirs]
            scores = mm(q, k, NT) * scale + open_ref[d]
            top = jnp.max(scores, axis=1, keepdims=True)
            expo = jnp.exp(scores - top)
            probs = expo * (1.0 / jnp.sum(expo, axis=1, keepdims=True))
            weights = probs.astype(BF16)
            attended = mm(weights, v, NN).astype(BF16)
            grad_ref[d, :, theirs] = mm(weights, g, TN).astype(BF16)
            dweights = mm(g, v, NT)
            delta = jnp.sum(probs * dweights, axis=1, keepdims=True)
            dscores = (probs * (dweights - delta) * scale).astype(BF16)
            query_grad = mm(dscores, k, NN).astype(BF16)
            grad_ref[d, :, mine] = mm(dscores, q, TN).astype(BF16)
            if d:
                back_ref[:, mine], back_ref[:, theirs] = attended, query_grad
            else:
                att_ref[:, mine], qg_ref[:, mine] = attended, query_grad
        for u in range(shards):
            for m in range(2):
                part = grad_ref[d, u * window : (u + 1) * window, m * gw : (m + 1) * gw]
                outs[m][u // 2][pl.ds(bases[u], window), :] += part


def attend(window, at, table, own, pair, keys, values):
    rows, width = own.shape
    gw = width // 2
    chips = len(keys)
    keys_n = 2 * chips * window
    half = jax.ShapeDtypeStruct((rows, gw), BF16)
    both = jax.ShapeDtypeStruct((rows, width), BF16)
    block = keys[0].shape
    return pl.pallas_call(
        functools.partial(attend_kernel, chips, window),
        grid_spec=pltpu.PrefetchScalarGridSpec(
            num_scalar_prefetch=2,
            grid=(1,),
            in_specs=[whole((rows, width))] * 2 + [whole(keys[0].shape)] * (2 * chips),
            out_specs=[whole((rows, gw))] * 2 + [whole((rows, width))] + [whole(block)] * (2 * chips),
            scratch_shapes=[
                pltpu.VMEM((2, rows, keys_n), F32),
                pltpu.VMEM((2, keys_n, width), BF16),
                pltpu.VMEM((2, keys_n, width), BF16),
            ],
        ),
        out_shape=[half, half, both] + [jax.ShapeDtypeStruct(block, BF16)] * (2 * chips),
        compiler_params=params(20 if keys_n <= 640 else 28),
        cost_estimate=cost(24 * rows * keys_n * gw, 8 * rows * width + 4 * keys_n * width, 4 * rows * keys_n),
    )(at, table, own, pair, *keys, *values)


def back_kernel(r, chunks, at, own_ref, other_ref, kw_ref, vw_ref, out_ref, w_ref, turned_ref, sems):
    depth, rows = out_ref.shape
    gw = own_ref.shape[1] // 2
    tile = min(TILE, depth)
    steps = depth // tile
    first = lax.rem(at[1] + r, chunks) * depth
    copies = []
    for n in range(steps):
        for m, ref in enumerate((kw_ref, vw_ref)):
            place = pl.ds(pl.multiple_of(first + n * tile, tile), tile)
            copies.append(pltpu.make_async_copy(ref.at[place, :], w_ref.at[m, n], sems.at[m, n]))
            copies[-1].start()
    for n, ref in enumerate((own_ref, other_ref)):
        start = pl.multiple_of(((at[0] & 1) ^ n) * gw, gw)
        for m in range(2):
            turned_ref[m, pl.ds(start, gw), :] = ref[:, m * gw : (m + 1) * gw].astype(F32).T.astype(BF16)
    for n in range(steps):
        copies[2 * n].wait()
        copies[2 * n + 1].wait()
        total = mm(w_ref[0, n], turned_ref[0], NN) + mm(w_ref[1, n], turned_ref[1], NN)
        out_ref[n * tile : (n + 1) * tile, :] = total.astype(BF16)


def project_back(r, chunks, at, own, other, key_weight, value_weight):
    rows, width = own.shape
    rows, gw = rows // 2, width // 2
    depth = key_weight.shape[0] // chunks
    tile = min(TILE, depth)
    steps = depth // tile
    row_spec = pl.BlockSpec((rows, width), lambda n, at: (at[0] & 1, 0))
    return pl.pallas_call(
        functools.partial(back_kernel, r, chunks),
        grid_spec=pltpu.PrefetchScalarGridSpec(
            num_scalar_prefetch=1,
            grid=(1,),
            in_specs=[row_spec] * 2 + [pl.BlockSpec(memory_space=pltpu.HBM)] * 2,
            out_specs=whole((depth, rows)),
            scratch_shapes=[
                pltpu.VMEM((2, steps, tile, 2 * gw), BF16),
                pltpu.VMEM((2, 2 * gw, rows), BF16),
                pltpu.SemaphoreType.DMA((2, steps)),
            ],
        ),
        out_shape=jax.ShapeDtypeStruct((depth, rows), BF16),
        compiler_params=params(48),
        cost_estimate=cost(8 * rows * gw * depth, 8 * gw * depth),
    )(at, own, other, key_weight, value_weight)


def weight_grad_kernel(chips, at, col_ref, *refs):
    grads = refs[: 4 * chips]
    outs = refs[4 * chips : -1]
    grad_ref = refs[-1]
    rows = grads[0].shape[0]
    half = pl.program_id(0) // (pl.num_programs(0) // 2)
    for m in range(2):

        @pl.when(half == m)
        def _():
            for n, out in enumerate(outs):
                for j in range(chips):
                    grad_ref[n, j * rows : (j + 1) * rows, :] = grads[(2 * m + n) * chips + j][...]
                out[...] = mm(col_ref[...], grad_ref[n], NN)


def weight_grads(at, cols, owns, others):
    chips = len(owns)
    rows, width = owns[0].shape
    gw = width // 2
    size = cols.shape[0]
    steps = gw // TILE
    arrays, specs = [], []
    for blocks, column in (
        (owns, lambda n: jnp.minimum(n, steps - 1)),
        (others, lambda n: jnp.maximum(n - steps, 0)),
    ):
        for half in range(2):
            for block in blocks:
                split = isinstance(block, tuple)
                first = 0 if split else half * steps
                arrays.append(block[half] if split else block)
                specs.append(pl.BlockSpec((rows, TILE), lambda n, at, f=first, c=column: (0, f + c(n))))
    out_spec = pl.BlockSpec((size, TILE), lambda n, at: (0, (n // steps ^ (at[0] & 1)) * steps + n % steps))
    return pl.pallas_call(
        functools.partial(weight_grad_kernel, chips),
        grid_spec=pltpu.PrefetchScalarGridSpec(
            num_scalar_prefetch=1,
            grid=(2 * steps,),
            in_specs=[whole(cols.shape)] + specs,
            out_specs=[out_spec] * 2,
            scratch_shapes=[pltpu.VMEM((2, chips * rows, TILE), BF16)],
        ),
        out_shape=[jax.ShapeDtypeStruct((size, width), F32)] * 2,
        compiler_params=params(16 if chips <= 4 else 28),
        cost_estimate=cost(4 * chips * rows * size * width, 2 * chips * rows * (size + 2 * width) + 8 * size * width),
    )(at, cols, *arrays)


def window_table(dp, enc_len, route, dec_len, window):
    shards = enc_len.shape[1]
    packed_rows = jnp.concatenate([enc_len, route, dec_len], axis=1)
    everyone = lax.all_to_all(
        jnp.broadcast_to(packed_rows, (shards, 3 * shards)), "dp", split_axis=0, concat_axis=0, tiled=True
    )
    lens, targets, decs = everyone[:, :shards], everyone[:, shards : 2 * shards], everyone[:, 2 * shards :]
    order = jnp.arange(shards, dtype=jnp.int32)
    before = (order[None, :] < order[:, None])[None]
    starts = jnp.sum(jnp.where(before, lens[:, None, :], 0), axis=2, dtype=jnp.int32)
    here = dp ^ jnp.arange(2, dtype=jnp.int32)
    hit = targets[None] == here[:, None, None]
    start = jnp.sum(jnp.where(hit, starts[None], 0), axis=2, dtype=jnp.int32)
    length = jnp.sum(jnp.where(hit, lens[None], 0), axis=2, dtype=jnp.int32)
    mine = jnp.sum(jnp.where((order[None] == here[:, None])[:, :, None], decs[None], 0), axis=1, dtype=jnp.int32)
    begin = jnp.sum(jnp.where(before, mine[:, None, :], 0), axis=2, dtype=jnp.int32)
    return start, length, begin


def body(queries, enc_rows, key_weight, value_weight, enc_len, dec_len, route, out_grad):
    shards = lax.axis_size("dp")
    peers = lax.axis_size("mp")
    chips = shards // 2
    packed = enc_rows.shape[0]
    window = 4 * packed // shards + 16
    gw = key_weight.shape[1] // 2
    dp, mp = lax.axis_index("dp"), lax.axis_index("mp")
    core = dp & 1
    at = jnp.stack([dp, mp]).astype(jnp.int32)

    def flip(x, r):
        return lax.ppermute(x, "dp", [(i, i ^ r) for i in range(shards)])

    def shift(x, r):
        return lax.ppermute(x, "mp", [(i, (i + r) % peers) for i in range(peers)])

    low = 1 << ((chips.bit_length() - 1) // 2)
    lows, highs = range(1, low), range(low, chips, low)

    def spread(x, low_first):
        got = {0: x}
        first, second = (lows, highs) if low_first else (highs, lows)
        for a in first:
            got[a] = flip(x, 2 * a)
        for b in second:
            got[b] = flip(x, 2 * b)
        for a in first:
            for b in second:
                got[a + b] = flip(got[a], 2 * b)
        return [got[j] for j in range(chips)]

    def collect(parts, low_first):
        first, second = (lows, highs) if low_first else (highs, lows)
        sums = {}
        for b in [*second, 0]:
            sums[b] = functools.reduce(jnp.add, [parts[b]] + [flip(parts[a + b], 2 * a) for a in first])
        return functools.reduce(jnp.add, [flip(sums[b], 2 * b) for b in second] + [sums[0]])

    def half_of(x, which):
        return lax.dynamic_slice_in_dim(x, which * gw, gw, axis=1)

    partner = flip(enc_rows, 1)
    owns = [enc_rows] + [shift(enc_rows, r) for r in range(1, peers)]
    mine, theirs = (jnp.concatenate([half_of(queries, c), half_of(out_grad, c)], axis=1) for c in (core, 1 - core))
    pair = flip(theirs, 1)
    start, length, begin = window_table(dp, enc_len, route, dec_len, window)
    base = jnp.minimum(start // 16 * 16, packed - window)
    table = jnp.stack([base, start - base, start - base + length, begin])
    sums = project(0, at, key_weight, value_weight, [enc_rows], [partner])
    sums, table, mine, pair, owns = lax.optimization_barrier((sums, table, mine, pair, owns))
    partners = [partner] + [flip(x, 1) for x in owns[1:]]
    keys, values = project(1, at, key_weight, value_weight, owns[1:], partners[1:], sums)
    keys, values = spread(keys, True), spread(values, False)
    cols = split_columns(chips, at, owns, partners)
    keys, values, cols = lax.optimization_barrier((keys, values, list(cols)))
    cols = [cols[0]] + [flip(cols[j], 2 * j) for j in range(1, chips)]
    attended, query_grad, back, *parts = attend(window, at, table, mine, pair, keys, values)
    parts, back, cols = lax.optimization_barrier((parts, back, cols))
    own = jnp.concatenate([collect(parts[:chips], False), collect(parts[chips:], True)], axis=1)
    back = flip(back, 1)
    outs = []
    for here, rest in ((attended, back[:, :gw]), (query_grad, back[:, gw:])):
        outs.append(jnp.where(core == 0, jnp.concatenate([here, rest], 1), jnp.concatenate([rest, here], 1)))
    cols = jnp.concatenate(cols, axis=1)
    own, cols = lax.optimization_barrier((own, cols))
    other = flip(own, 1)
    middle = peers // 2
    order = [middle] + [r for r in range(1, peers) if r != middle] + [0]
    chunks = [project_back(r, peers, at, own, other, key_weight, value_weight) for r in order]
    arrived = [shift(x, r) for x, r in zip(chunks[:-1], order)]
    owns = {0: own}
    for j in [*lows, *highs]:
        owns[j] = flip(own, 2 * j)
    owns, _ = lax.optimization_barrier((owns, chunks[:-1]))
    for a in lows:
        for b in highs:
            owns[a + b] = (flip(owns[a][:, :gw], 2 * b), flip(owns[b][:, gw:], 2 * a))
    owns = [owns[j] for j in range(chips)]
    owns, arrived[:2], chunk, outs = lax.optimization_barrier((owns, arrived[:2], chunks[-1], outs))
    others = [other] + [tuple(flip(y, 1) for y in x) if isinstance(x, tuple) else flip(x, 1) for x in owns[1:]]
    weight_out = weight_grads(at, cols, owns, others)
    arrived, weight_out = lax.optimization_barrier((arrived, weight_out))
    total = functools.reduce(jnp.add, [x.astype(F32) for x in [chunk, *arrived]])
    return (*outs, total.T.astype(BF16), *weight_out)


def solution(mesh):
    in_specs = (
        P("dp", "mp"),
        P("dp", "mp"),
        P(None, "mp"),
        P(None, "mp"),
        P("dp", None),
        P("dp", None),
        P("dp", None),
        P("dp", "mp"),
    )
    out_specs = (P("dp", "mp"), P("dp", "mp"), P("dp", "mp"), P("dp", "mp"), P("dp", "mp"))
    return jax.shard_map(body, mesh=mesh, in_specs=in_specs, out_specs=out_specs, check_vma=False)
```

```python
import functools

import jax
import jax.numpy as jnp
from jax import lax
from jax.experimental import pallas as pl
from jax.experimental.pallas import tpu as pltpu
from jax.sharding import PartitionSpec as P

HD = 256
TILE = 256
NT = (((1,), (1,)), ((), ()))
NN = (((1,), (0,)), ((), ()))
TN = (((0,), (0,)), ((), ()))
SMEM = pl.BlockSpec(memory_space=pltpu.SMEM)
BF16 = jnp.bfloat16
F32 = jnp.float32


def mm(a, b, dims):
    return lax.dot_general(a, b, dims, preferred_element_type=F32)


def params(mib=60):
    return pltpu.CompilerParams(vmem_limit_bytes=mib * 2**20)


def cost(flops, nbytes, exps=0):
    return pl.CostEstimate(flops=flops // 1024, bytes_accessed=nbytes // 1024, transcendentals=exps // 1024)


def whole(shape):
    return pl.BlockSpec(shape, lambda *_: (0,) * len(shape))


def pair_rows(ref, core, own, partner):
    rows = own.shape[0]
    ref[pl.ds(pl.multiple_of(core * rows, rows), rows), :] = own
    ref[pl.ds(pl.multiple_of((1 - core) * rows, rows), rows), :] = partner


def project_kernel(first, blocks, cuts, final, at, kw_ref, vw_ref, *refs):
    owns, partners = refs[:blocks], refs[blocks : 2 * blocks]
    enc_ref, acc_ref, w_ref, sems = refs[-4:]
    _, steps, tile, gw = w_ref.shape
    peers = kw_ref.shape[0] // (cuts * tile)
    core = at[0] & 1
    copies = []
    for n in range(steps):
        block = lax.rem(at[1] + 2 * peers - first - n // cuts, peers)
        rows = pl.ds(pl.multiple_of((block * cuts + n % cuts) * tile, tile), tile)
        cols = pl.ds(pl.multiple_of(core * gw, gw), gw)
        for m, ref in enumerate((kw_ref, vw_ref)):
            copies.append(pltpu.make_async_copy(ref.at[rows, cols], w_ref.at[m, n], sems.at[m, n]))
            copies[-1].start()
    for n in range(steps):
        place = slice(n % cuts * tile, (n % cuts + 1) * tile)
        pair_rows(enc_ref.at[n], core, owns[n // cuts][:, place], partners[n // cuts][:, place])
    acc_ref[...] = refs[2 * blocks][...] if final else jnp.zeros_like(acc_ref)
    for n in range(steps):
        copies[2 * n].wait()
        copies[2 * n + 1].wait()
        acc_ref[:, :gw] += mm(enc_ref[n], w_ref[0, n], NN)
        acc_ref[:, gw:] += mm(enc_ref[n], w_ref[1, n], NN)
    if final:
        refs[-6][...] = acc_ref[:, :gw].astype(BF16)
        refs[-5][...] = acc_ref[:, gw:].astype(BF16)
    else:
        refs[-5][...] = acc_ref[...]


def project(first, at, key_weight, value_weight, owns, partners, sums=None):
    rows, depth = owns[0].shape
    gw = key_weight.shape[1] // 2
    blocks = len(owns)
    final = sums is not None
    cuts = 2
    tile = depth // cuts
    out_shape = (2 * rows, 2 * gw)
    half = (2 * rows, gw)
    return pl.pallas_call(
        functools.partial(project_kernel, first, blocks, cuts, final),
        grid_spec=pltpu.PrefetchScalarGridSpec(
            num_scalar_prefetch=1,
            grid=(1,),
            in_specs=[pl.BlockSpec(memory_space=pltpu.HBM)] * 2
            + [whole((rows, depth))] * (2 * blocks)
            + [whole(out_shape)] * final,
            out_specs=[whole(half)] * 2 if final else whole(out_shape),
            scratch_shapes=[
                pltpu.VMEM((blocks * cuts, 2 * rows, tile), BF16),
                pltpu.VMEM(out_shape, F32),
                pltpu.VMEM((2, blocks * cuts, tile, gw), BF16),
                pltpu.SemaphoreType.DMA((2, blocks * cuts)),
            ],
        ),
        out_shape=[jax.ShapeDtypeStruct(half, BF16)] * 2 if final else jax.ShapeDtypeStruct(out_shape, F32),
        compiler_params=params(48),
        cost_estimate=cost(8 * blocks * rows * depth * gw, 4 * blocks * depth * gw),
    )(at, key_weight, value_weight, *owns, *partners, *([sums] if final else []))


def split_kernel(peers, at, *refs):
    owns, partners = refs[:peers], refs[peers : 2 * peers]
    outs, all_ref = refs[2 * peers : -1], refs[-1]
    size = outs[0].shape[0]
    per = owns[0].shape[1] // size
    for r in range(peers):
        for c in range(per):
            place = slice(c * size, (c + 1) * size)
            pair_rows(all_ref.at[r * per + c], at[0] & 1, owns[r][:, place], partners[r][:, place])
    for j, out in enumerate(outs):
        target = at[0] ^ (2 * j)
        r = lax.rem(at[1] + peers - lax.div(target, per), peers)
        out[...] = all_ref[r * per + lax.rem(target, per)].astype(F32).T.astype(BF16)


def split_columns(chips, at, owns, partners):
    rows, depth = owns[0].shape
    peers = len(owns)
    size = peers * depth // (2 * chips)
    return pl.pallas_call(
        functools.partial(split_kernel, peers),
        grid_spec=pltpu.PrefetchScalarGridSpec(
            num_scalar_prefetch=1,
            grid=(1,),
            in_specs=[whole((rows, depth))] * (2 * peers),
            out_specs=[whole((size, 2 * rows))] * chips,
            scratch_shapes=[pltpu.VMEM((2 * chips, 2 * rows, size), BF16)],
        ),
        out_shape=[jax.ShapeDtypeStruct((size, 2 * rows), BF16)] * chips,
        compiler_params=params(16),
        cost_estimate=cost(0, 8 * peers * rows * depth),
    )(at, *owns, *partners)


def attend_kernel(chips, window, at, table, own_ref, pair_ref, *refs):
    keys, values = refs[:chips], refs[chips : 2 * chips]
    att_ref, qg_ref, back_ref = refs[2 * chips : 2 * chips + 3]
    outs = refs[2 * chips + 3 : -3]
    outs = (outs[:chips], outs[chips:])
    open_ref, key_ref, grad_ref = refs[-3:]
    rows, gw = att_ref.shape
    shards = 2 * chips
    packed = keys[0].shape[0] // 2
    keys_n = shards * window
    scale = HD ** (-0.5)
    for out in outs[0] + outs[1]:
        out[...] = jnp.zeros_like(out)
    for d in range(2):
        row = lax.broadcasted_iota(jnp.int32, (rows, 128), 0)
        low = jnp.zeros((rows, 128), jnp.int32)
        high = jnp.zeros((rows, 128), jnp.int32)
        for s in range(shards):
            place = (s ^ (at[0] & -2)) * window
            low = jnp.where(row >= table[3, d, s], place + table[1, d, s], low)
            high = jnp.where(row >= table[3, d, s], place + table[2, d, s], high)
        for c in range(0, keys_n, 128):
            col = lax.broadcasted_iota(jnp.int32, (rows, 128), 1) + c
            open_ref[d, :, c : c + 128] = jnp.where((col >= low) & (col < high), 0.0, -jnp.inf)
        bases = []
        for u in range(shards):
            bases.append(pl.multiple_of(u % 2 * packed + table[0, d, u ^ (at[0] & -2)], 16))
            key_ref[d, u * window : (u + 1) * window, :gw] = keys[u // 2][pl.ds(bases[u], window), :]
            key_ref[d, u * window : (u + 1) * window, gw:] = values[u // 2][pl.ds(bases[u], window), :]
        for h in range(gw // HD):
            mine = slice(h * HD, (h + 1) * HD)
            theirs = slice(gw + h * HD, gw + (h + 1) * HD)
            q, g = ((own_ref, pair_ref)[d][:, place] for place in (mine, theirs))
            k, v = key_ref[d, :, mine], key_ref[d, :, theirs]
            scores = mm(q, k, NT) * scale + open_ref[d]
            top = jnp.max(scores, axis=1, keepdims=True)
            expo = jnp.exp(scores - top)
            probs = expo * (1.0 / jnp.sum(expo, axis=1, keepdims=True))
            weights = probs.astype(BF16)
            attended = mm(weights, v, NN).astype(BF16)
            grad_ref[d, :, theirs] = mm(weights, g, TN).astype(BF16)
            dweights = mm(g, v, NT)
            delta = jnp.sum(probs * dweights, axis=1, keepdims=True)
            dscores = (probs * (dweights - delta) * scale).astype(BF16)
            query_grad = mm(dscores, k, NN).astype(BF16)
            grad_ref[d, :, mine] = mm(dscores, q, TN).astype(BF16)
            if d:
                back_ref[:, mine], back_ref[:, theirs] = attended, query_grad
            else:
                att_ref[:, mine], qg_ref[:, mine] = attended, query_grad
        for u in range(shards):
            for m in range(2):
                part = grad_ref[d, u * window : (u + 1) * window, m * gw : (m + 1) * gw]
                outs[m][u // 2][pl.ds(bases[u], window), :] += part


def attend(window, at, table, own, pair, keys, values):
    rows, width = own.shape
    gw = width // 2
    chips = len(keys)
    keys_n = 2 * chips * window
    half = jax.ShapeDtypeStruct((rows, gw), BF16)
    both = jax.ShapeDtypeStruct((rows, width), BF16)
    block = keys[0].shape
    return pl.pallas_call(
        functools.partial(attend_kernel, chips, window),
        grid_spec=pltpu.PrefetchScalarGridSpec(
            num_scalar_prefetch=2,
            grid=(1,),
            in_specs=[whole((rows, width))] * 2 + [whole(keys[0].shape)] * (2 * chips),
            out_specs=[whole((rows, gw))] * 2 + [whole((rows, width))] + [whole(block)] * (2 * chips),
            scratch_shapes=[
                pltpu.VMEM((2, rows, keys_n), F32),
                pltpu.VMEM((2, keys_n, width), BF16),
                pltpu.VMEM((2, keys_n, width), BF16),
            ],
        ),
        out_shape=[half, half, both] + [jax.ShapeDtypeStruct(block, BF16)] * (2 * chips),
        compiler_params=params(20 if keys_n <= 640 else 28),
        cost_estimate=cost(24 * rows * keys_n * gw, 8 * rows * width + 4 * keys_n * width, 4 * rows * keys_n),
    )(at, table, own, pair, *keys, *values)


def back_kernel(places, chunks, at, own_ref, other_ref, kw_ref, vw_ref, *refs):
    outs = refs[: len(places)]
    w_ref, turned_ref, sems = refs[len(places) :]
    depth, rows = outs[0].shape
    gw = own_ref.shape[1] // 2
    tile = min(TILE, depth)
    steps = depth // tile
    copies = []
    for c, r in enumerate(places):
        first = lax.rem(at[1] + r, chunks) * depth
        for n in range(steps):
            for m, ref in enumerate((kw_ref, vw_ref)):
                place = pl.ds(pl.multiple_of(first + n * tile, tile), tile)
                step = c * steps + n
                copies.append(pltpu.make_async_copy(ref.at[place, :], w_ref.at[m, step], sems.at[m, step]))
                copies[-1].start()
    for n, ref in enumerate((own_ref, other_ref)):
        start = pl.multiple_of(((at[0] & 1) ^ n) * gw, gw)
        for m in range(2):
            turned_ref[m, pl.ds(start, gw), :] = ref[:, m * gw : (m + 1) * gw].astype(F32).T.astype(BF16)
    for step in range(len(places) * steps):
        copies[2 * step].wait()
        copies[2 * step + 1].wait()
        total = mm(w_ref[0, step], turned_ref[0], NN) + mm(w_ref[1, step], turned_ref[1], NN)
        n = step % steps
        outs[step // steps][n * tile : (n + 1) * tile, :] = total.astype(BF16)


def project_back(places, chunks, at, own, other, key_weight, value_weight):
    rows, width = own.shape
    rows, gw = rows // 2, width // 2
    depth = key_weight.shape[0] // chunks
    tile = min(TILE, depth)
    steps = len(places) * (depth // tile)
    row_spec = pl.BlockSpec((rows, width), lambda n, at: (at[0] & 1, 0))
    return pl.pallas_call(
        functools.partial(back_kernel, places, chunks),
        grid_spec=pltpu.PrefetchScalarGridSpec(
            num_scalar_prefetch=1,
            grid=(1,),
            in_specs=[row_spec] * 2 + [pl.BlockSpec(memory_space=pltpu.HBM)] * 2,
            out_specs=[whole((depth, rows))] * len(places),
            scratch_shapes=[
                pltpu.VMEM((2, steps, tile, 2 * gw), BF16),
                pltpu.VMEM((2, 2 * gw, rows), BF16),
                pltpu.SemaphoreType.DMA((2, steps)),
            ],
        ),
        out_shape=[jax.ShapeDtypeStruct((depth, rows), BF16)] * len(places),
        compiler_params=params(48),
        cost_estimate=cost(8 * rows * gw * depth, 8 * gw * depth),
    )(at, own, other, key_weight, value_weight)


def weight_grad_kernel(chips, at, col_ref, *refs):
    grads = refs[: 4 * chips]
    outs = refs[4 * chips : -1]
    grad_ref = refs[-1]
    rows = grads[0].shape[0]
    half = pl.program_id(0) // (pl.num_programs(0) // 2)
    for m in range(2):

        @pl.when(half == m)
        def _():
            for n, out in enumerate(outs):
                for j in range(chips):
                    grad_ref[n, j * rows : (j + 1) * rows, :] = grads[(2 * m + n) * chips + j][...]
                out[...] = mm(col_ref[...], grad_ref[n], NN)


def weight_grads(at, cols, owns, others):
    chips = len(owns)
    rows, width = owns[0].shape
    gw = width // 2
    size = cols.shape[0]
    steps = gw // TILE
    arrays, specs = [], []
    for blocks, column in (
        (owns, lambda n: jnp.minimum(n, steps - 1)),
        (others, lambda n: jnp.maximum(n - steps, 0)),
    ):
        for half in range(2):
            for block in blocks:
                split = isinstance(block, tuple)
                first = 0 if split else half * steps
                arrays.append(block[half] if split else block)
                specs.append(pl.BlockSpec((rows, TILE), lambda n, at, f=first, c=column: (0, f + c(n))))
    out_spec = pl.BlockSpec((size, TILE), lambda n, at: (0, (n // steps ^ (at[0] & 1)) * steps + n % steps))
    return pl.pallas_call(
        functools.partial(weight_grad_kernel, chips),
        grid_spec=pltpu.PrefetchScalarGridSpec(
            num_scalar_prefetch=1,
            grid=(2 * steps,),
            in_specs=[whole(cols.shape)] + specs,
            out_specs=[out_spec] * 2,
            scratch_shapes=[pltpu.VMEM((2, chips * rows, TILE), BF16)],
        ),
        out_shape=[jax.ShapeDtypeStruct((size, width), F32)] * 2,
        compiler_params=params(16 if chips <= 4 else 28),
        cost_estimate=cost(4 * chips * rows * size * width, 2 * chips * rows * (size + 2 * width) + 8 * size * width),
    )(at, cols, *arrays)


def window_table(dp, enc_len, route, dec_len, window):
    shards = enc_len.shape[1]
    packed_rows = jnp.concatenate([enc_len, route, dec_len], axis=1)
    everyone = lax.all_to_all(
        jnp.broadcast_to(packed_rows, (shards, 3 * shards)), "dp", split_axis=0, concat_axis=0, tiled=True
    )
    lens, targets, decs = everyone[:, :shards], everyone[:, shards : 2 * shards], everyone[:, 2 * shards :]
    order = jnp.arange(shards, dtype=jnp.int32)
    before = (order[None, :] < order[:, None])[None]
    starts = jnp.sum(jnp.where(before, lens[:, None, :], 0), axis=2, dtype=jnp.int32)
    here = dp ^ jnp.arange(2, dtype=jnp.int32)
    hit = targets[None] == here[:, None, None]
    start = jnp.sum(jnp.where(hit, starts[None], 0), axis=2, dtype=jnp.int32)
    length = jnp.sum(jnp.where(hit, lens[None], 0), axis=2, dtype=jnp.int32)
    mine = jnp.sum(jnp.where((order[None] == here[:, None])[:, :, None], decs[None], 0), axis=1, dtype=jnp.int32)
    begin = jnp.sum(jnp.where(before, mine[:, None, :], 0), axis=2, dtype=jnp.int32)
    return start, length, begin


def body(queries, enc_rows, key_weight, value_weight, enc_len, dec_len, route, out_grad):
    shards = lax.axis_size("dp")
    peers = lax.axis_size("mp")
    chips = shards // 2
    packed = enc_rows.shape[0]
    window = 4 * packed // shards + 16
    gw = key_weight.shape[1] // 2
    dp, mp = lax.axis_index("dp"), lax.axis_index("mp")
    core = dp & 1
    at = jnp.stack([dp, mp]).astype(jnp.int32)

    def flip(x, r):
        return lax.ppermute(x, "dp", [(i, i ^ r) for i in range(shards)])

    def shift(x, r):
        return lax.ppermute(x, "mp", [(i, (i + r) % peers) for i in range(peers)])

    low = 1 << ((chips.bit_length() - 1) // 2)
    lows, highs = range(1, low), range(low, chips, low)

    def spread(x, low_first):
        got = {0: x}
        first, second = (lows, highs) if low_first else (highs, lows)
        for a in first:
            got[a] = flip(x, 2 * a)
        for b in second:
            got[b] = flip(x, 2 * b)
        for a in first:
            for b in second:
                got[a + b] = flip(got[a], 2 * b)
        return [got[j] for j in range(chips)]

    def collect(parts, low_first):
        first, second = (lows, highs) if low_first else (highs, lows)
        sums = {}
        for b in [*second, 0]:
            sums[b] = functools.reduce(jnp.add, [parts[b]] + [flip(parts[a + b], 2 * a) for a in first])
        return functools.reduce(jnp.add, [flip(sums[b], 2 * b) for b in second] + [sums[0]])

    def half_of(x, which):
        return lax.dynamic_slice_in_dim(x, which * gw, gw, axis=1)

    partner = flip(enc_rows, 1)
    owns = [enc_rows] + [shift(enc_rows, r) for r in range(1, peers)]
    mine, theirs = (jnp.concatenate([half_of(queries, c), half_of(out_grad, c)], axis=1) for c in (core, 1 - core))
    pair = flip(theirs, 1)
    start, length, begin = window_table(dp, enc_len, route, dec_len, window)
    base = jnp.minimum(start // 16 * 16, packed - window)
    table = jnp.stack([base, start - base, start - base + length, begin])
    sums = project(0, at, key_weight, value_weight, [enc_rows], [partner])
    sums, table, mine, pair, owns = lax.optimization_barrier((sums, table, mine, pair, owns))
    partners = [partner] + [flip(x, 1) for x in owns[1:]]
    keys, values = project(1, at, key_weight, value_weight, owns[1:], partners[1:], sums)
    keys, values = spread(keys, True), spread(values, False)
    cols = split_columns(chips, at, owns, partners)
    keys, values, cols = lax.optimization_barrier((keys, values, list(cols)))
    cols = [cols[0]] + [flip(cols[j], 2 * j) for j in range(1, chips)]
    attended, query_grad, back, *parts = attend(window, at, table, mine, pair, keys, values)
    parts, back, cols = lax.optimization_barrier((parts, back, cols))
    own = jnp.concatenate([collect(parts[:chips], False), collect(parts[chips:], True)], axis=1)
    back = flip(back, 1)
    outs = []
    for here, rest in ((attended, back[:, :gw]), (query_grad, back[:, gw:])):
        outs.append(jnp.where(core == 0, jnp.concatenate([here, rest], 1), jnp.concatenate([rest, here], 1)))
    cols = jnp.concatenate(cols, axis=1)
    own, cols = lax.optimization_barrier((own, cols))
    other = flip(own, 1)
    owns = {0: own}
    for j in [*lows, *highs]:
        owns[j] = flip(own, 2 * j)
    middle = peers // 2
    rest = [r for r in range(1, peers) if r != middle]
    chunks = list(project_back((middle,), peers, at, own, other, key_weight, value_weight))
    arrived = [shift(chunks[0], middle)]
    chunks += list(project_back((*rest, 0), peers, at, own, other, key_weight, value_weight))
    arrived += [shift(x, r) for x, r in zip(chunks[1:-1], rest)]
    owns, _ = lax.optimization_barrier((owns, chunks[:-1]))
    for a in lows:
        for b in highs:
            owns[a + b] = (flip(owns[a][:, :gw], 2 * b), flip(owns[b][:, gw:], 2 * a))
    owns = [owns[j] for j in range(chips)]
    owns, arrived[:2], chunk, outs = lax.optimization_barrier((owns, arrived[:2], chunks[-1], outs))
    others = [other] + [tuple(flip(y, 1) for y in x) if isinstance(x, tuple) else flip(x, 1) for x in owns[1:]]
    weight_out = weight_grads(at, cols, owns, others)
    arrived, weight_out = lax.optimization_barrier((arrived, weight_out))
    total = functools.reduce(jnp.add, [x.astype(F32) for x in [chunk, *arrived]])
    return (*outs, total.T.astype(BF16), *weight_out)


def solution(mesh):
    in_specs = (
        P("dp", "mp"),
        P("dp", "mp"),
        P(None, "mp"),
        P(None, "mp"),
        P("dp", None),
        P("dp", None),
        P("dp", None),
        P("dp", "mp"),
    )
    out_specs = (P("dp", "mp"), P("dp", "mp"), P("dp", "mp"), P("dp", "mp"), P("dp", "mp"))
    return jax.shard_map(body, mesh=mesh, in_specs=in_specs, out_specs=out_specs, check_vma=False)
```

```python
import functools

import jax
import jax.numpy as jnp
from jax import lax
from jax.experimental import pallas as pl
from jax.experimental.pallas import tpu as pltpu
from jax.sharding import PartitionSpec as P

HD = 256
TILE = 256
NT = (((1,), (1,)), ((), ()))
NN = (((1,), (0,)), ((), ()))
TN = (((0,), (0,)), ((), ()))
SMEM = pl.BlockSpec(memory_space=pltpu.SMEM)
BF16 = jnp.bfloat16
F32 = jnp.float32


def mm(a, b, dims):
    return lax.dot_general(a, b, dims, preferred_element_type=F32)


def params(mib=60):
    return pltpu.CompilerParams(vmem_limit_bytes=mib * 2**20)


def cost(flops, nbytes, exps=0):
    return pl.CostEstimate(flops=flops // 1024, bytes_accessed=nbytes // 1024, transcendentals=exps // 1024)


def whole(shape):
    return pl.BlockSpec(shape, lambda *_: (0,) * len(shape))


def pair_rows(ref, core, own, partner):
    rows = own.shape[0]
    ref[pl.ds(pl.multiple_of(core * rows, rows), rows), :] = own
    ref[pl.ds(pl.multiple_of((1 - core) * rows, rows), rows), :] = partner


def project_kernel(first, blocks, cuts, final, at, kw_ref, vw_ref, *refs):
    owns, partners = refs[:blocks], refs[blocks : 2 * blocks]
    enc_ref, acc_ref, w_ref, sems = refs[-4:]
    _, steps, tile, gw = w_ref.shape
    peers = kw_ref.shape[0] // (cuts * tile)
    core = at[0] & 1
    copies = []
    for n in range(steps):
        block = lax.rem(at[1] + 2 * peers - first - n // cuts, peers)
        rows = pl.ds(pl.multiple_of((block * cuts + n % cuts) * tile, tile), tile)
        cols = pl.ds(pl.multiple_of(core * gw, gw), gw)
        for m, ref in enumerate((kw_ref, vw_ref)):
            copies.append(pltpu.make_async_copy(ref.at[rows, cols], w_ref.at[m, n], sems.at[m, n]))
            copies[-1].start()
    for n in range(steps):
        place = slice(n % cuts * tile, (n % cuts + 1) * tile)
        pair_rows(enc_ref.at[n], core, owns[n // cuts][:, place], partners[n // cuts][:, place])
    acc_ref[...] = refs[2 * blocks][...] if final else jnp.zeros_like(acc_ref)
    for n in range(steps):
        copies[2 * n].wait()
        copies[2 * n + 1].wait()
        acc_ref[:, :gw] += mm(enc_ref[n], w_ref[0, n], NN)
        acc_ref[:, gw:] += mm(enc_ref[n], w_ref[1, n], NN)
    if final:
        refs[-6][...] = acc_ref[:, :gw].astype(BF16)
        refs[-5][...] = acc_ref[:, gw:].astype(BF16)
    else:
        refs[-5][...] = acc_ref[...]


def project(first, at, key_weight, value_weight, owns, partners, sums=None):
    rows, depth = owns[0].shape
    gw = key_weight.shape[1] // 2
    blocks = len(owns)
    final = sums is not None
    cuts = 2
    tile = depth // cuts
    out_shape = (2 * rows, 2 * gw)
    half = (2 * rows, gw)
    return pl.pallas_call(
        functools.partial(project_kernel, first, blocks, cuts, final),
        grid_spec=pltpu.PrefetchScalarGridSpec(
            num_scalar_prefetch=1,
            grid=(1,),
            in_specs=[pl.BlockSpec(memory_space=pltpu.HBM)] * 2
            + [whole((rows, depth))] * (2 * blocks)
            + [whole(out_shape)] * final,
            out_specs=[whole(half)] * 2 if final else whole(out_shape),
            scratch_shapes=[
                pltpu.VMEM((blocks * cuts, 2 * rows, tile), BF16),
                pltpu.VMEM(out_shape, F32),
                pltpu.VMEM((2, blocks * cuts, tile, gw), BF16),
                pltpu.SemaphoreType.DMA((2, blocks * cuts)),
            ],
        ),
        out_shape=[jax.ShapeDtypeStruct(half, BF16)] * 2 if final else jax.ShapeDtypeStruct(out_shape, F32),
        compiler_params=params(48),
        cost_estimate=cost(8 * blocks * rows * depth * gw, 4 * blocks * depth * gw),
    )(at, key_weight, value_weight, *owns, *partners, *([sums] if final else []))


def split_kernel(peers, at, *refs):
    owns, partners = refs[:peers], refs[peers : 2 * peers]
    outs, all_ref = refs[2 * peers : -1], refs[-1]
    size = outs[0].shape[0]
    per = owns[0].shape[1] // size
    for r in range(peers):
        for c in range(per):
            place = slice(c * size, (c + 1) * size)
            pair_rows(all_ref.at[r * per + c], at[0] & 1, owns[r][:, place], partners[r][:, place])
    for j, out in enumerate(outs):
        target = at[0] ^ (2 * j)
        r = lax.rem(at[1] + peers - lax.div(target, per), peers)
        out[...] = all_ref[r * per + lax.rem(target, per)].astype(F32).T.astype(BF16)


def split_columns(chips, at, owns, partners):
    rows, depth = owns[0].shape
    peers = len(owns)
    size = peers * depth // (2 * chips)
    return pl.pallas_call(
        functools.partial(split_kernel, peers),
        grid_spec=pltpu.PrefetchScalarGridSpec(
            num_scalar_prefetch=1,
            grid=(1,),
            in_specs=[whole((rows, depth))] * (2 * peers),
            out_specs=[whole((size, 2 * rows))] * chips,
            scratch_shapes=[pltpu.VMEM((2 * chips, 2 * rows, size), BF16)],
        ),
        out_shape=[jax.ShapeDtypeStruct((size, 2 * rows), BF16)] * chips,
        compiler_params=params(16),
        cost_estimate=cost(0, 8 * peers * rows * depth),
    )(at, *owns, *partners)


def attend_kernel(chips, window, at, table, own_ref, pair_ref, *refs):
    keys, values = refs[:chips], refs[chips : 2 * chips]
    att_ref, qg_ref, back_ref = refs[2 * chips : 2 * chips + 3]
    outs = refs[2 * chips + 3 : -3]
    outs = (outs[:chips], outs[chips:])
    open_ref, key_ref, grad_ref = refs[-3:]
    rows, gw = att_ref.shape
    shards = 2 * chips
    packed = keys[0].shape[0] // 2
    keys_n = shards * window
    scale = HD ** (-0.5)
    for out in outs[0] + outs[1]:
        out[...] = jnp.zeros_like(out)
    for d in range(2):
        row = lax.broadcasted_iota(jnp.int32, (rows, 128), 0)
        low = jnp.zeros((rows, 128), jnp.int32)
        high = jnp.zeros((rows, 128), jnp.int32)
        for s in range(shards):
            place = (s ^ (at[0] & -2)) * window
            low = jnp.where(row >= table[3, d, s], place + table[1, d, s], low)
            high = jnp.where(row >= table[3, d, s], place + table[2, d, s], high)
        for c in range(0, keys_n, 128):
            col = lax.broadcasted_iota(jnp.int32, (rows, 128), 1) + c
            open_ref[d, :, c : c + 128] = jnp.where((col >= low) & (col < high), 0.0, -jnp.inf)
        bases = []
        for u in range(shards):
            bases.append(pl.multiple_of(u % 2 * packed + table[0, d, u ^ (at[0] & -2)], 16))
            key_ref[d, u * window : (u + 1) * window, :gw] = keys[u // 2][pl.ds(bases[u], window), :]
            key_ref[d, u * window : (u + 1) * window, gw:] = values[u // 2][pl.ds(bases[u], window), :]
        for h in range(gw // HD):
            mine = slice(h * HD, (h + 1) * HD)
            theirs = slice(gw + h * HD, gw + (h + 1) * HD)
            q, g = ((own_ref, pair_ref)[d][:, place] for place in (mine, theirs))
            k, v = key_ref[d, :, mine], key_ref[d, :, theirs]
            scores = mm(q, k, NT) * scale + open_ref[d]
            top = jnp.max(scores, axis=1, keepdims=True)
            expo = jnp.exp(scores - top)
            probs = expo * (1.0 / jnp.sum(expo, axis=1, keepdims=True))
            weights = probs.astype(BF16)
            attended = mm(weights, v, NN).astype(BF16)
            grad_ref[d, :, theirs] = mm(weights, g, TN).astype(BF16)
            dweights = mm(g, v, NT)
            delta = jnp.sum(probs * dweights, axis=1, keepdims=True)
            dscores = (probs * (dweights - delta) * scale).astype(BF16)
            query_grad = mm(dscores, k, NN).astype(BF16)
            grad_ref[d, :, mine] = mm(dscores, q, TN).astype(BF16)
            if d:
                back_ref[:, mine], back_ref[:, theirs] = attended, query_grad
            else:
                att_ref[:, mine], qg_ref[:, mine] = attended, query_grad
        for u in range(shards):
            for m in range(2):
                part = grad_ref[d, u * window : (u + 1) * window, m * gw : (m + 1) * gw]
                outs[m][u // 2][pl.ds(bases[u], window), :] += part


def attend(window, at, table, own, pair, keys, values):
    rows, width = own.shape
    gw = width // 2
    chips = len(keys)
    keys_n = 2 * chips * window
    half = jax.ShapeDtypeStruct((rows, gw), BF16)
    both = jax.ShapeDtypeStruct((rows, width), BF16)
    block = keys[0].shape
    return pl.pallas_call(
        functools.partial(attend_kernel, chips, window),
        grid_spec=pltpu.PrefetchScalarGridSpec(
            num_scalar_prefetch=2,
            grid=(1,),
            in_specs=[whole((rows, width))] * 2 + [whole(keys[0].shape)] * (2 * chips),
            out_specs=[whole((rows, gw))] * 2 + [whole((rows, width))] + [whole(block)] * (2 * chips),
            scratch_shapes=[
                pltpu.VMEM((2, rows, keys_n), F32),
                pltpu.VMEM((2, keys_n, width), BF16),
                pltpu.VMEM((2, keys_n, width), BF16),
            ],
        ),
        out_shape=[half, half, both] + [jax.ShapeDtypeStruct(block, BF16)] * (2 * chips),
        compiler_params=params(20 if keys_n <= 640 else 28),
        cost_estimate=cost(24 * rows * keys_n * gw, 8 * rows * width + 4 * keys_n * width, 4 * rows * keys_n),
    )(at, table, own, pair, *keys, *values)


def back_kernel(places, chunks, at, own_ref, other_ref, kw_ref, vw_ref, *refs):
    outs = refs[: len(places)]
    w_ref, turned_ref, sems = refs[len(places) :]
    depth, rows = outs[0].shape
    gw = own_ref.shape[1] // 2
    tile = min(TILE, depth)
    steps = depth // tile
    copies = []
    for c, r in enumerate(places):
        first = lax.rem(at[1] + r, chunks) * depth
        for n in range(steps):
            for m, ref in enumerate((kw_ref, vw_ref)):
                place = pl.ds(pl.multiple_of(first + n * tile, tile), tile)
                step = c * steps + n
                copies.append(pltpu.make_async_copy(ref.at[place, :], w_ref.at[m, step], sems.at[m, step]))
                copies[-1].start()
    for n, ref in enumerate((own_ref, other_ref)):
        start = pl.multiple_of(((at[0] & 1) ^ n) * gw, gw)
        for m in range(2):
            turned_ref[m, pl.ds(start, gw), :] = ref[:, m * gw : (m + 1) * gw].astype(F32).T.astype(BF16)
    for step in range(len(places) * steps):
        copies[2 * step].wait()
        copies[2 * step + 1].wait()
        total = mm(w_ref[0, step], turned_ref[0], NN) + mm(w_ref[1, step], turned_ref[1], NN)
        n = step % steps
        outs[step // steps][n * tile : (n + 1) * tile, :] = total.astype(BF16)


def project_back(places, chunks, at, own, other, key_weight, value_weight):
    rows, width = own.shape
    rows, gw = rows // 2, width // 2
    depth = key_weight.shape[0] // chunks
    tile = min(TILE, depth)
    steps = len(places) * (depth // tile)
    row_spec = pl.BlockSpec((rows, width), lambda n, at: (at[0] & 1, 0))
    return pl.pallas_call(
        functools.partial(back_kernel, places, chunks),
        grid_spec=pltpu.PrefetchScalarGridSpec(
            num_scalar_prefetch=1,
            grid=(1,),
            in_specs=[row_spec] * 2 + [pl.BlockSpec(memory_space=pltpu.HBM)] * 2,
            out_specs=[whole((depth, rows))] * len(places),
            scratch_shapes=[
                pltpu.VMEM((2, steps, tile, 2 * gw), BF16),
                pltpu.VMEM((2, 2 * gw, rows), BF16),
                pltpu.SemaphoreType.DMA((2, steps)),
            ],
        ),
        out_shape=[jax.ShapeDtypeStruct((depth, rows), BF16)] * len(places),
        compiler_params=params(48),
        cost_estimate=cost(8 * rows * gw * depth, 8 * gw * depth),
    )(at, own, other, key_weight, value_weight)


def weight_grad_kernel(chips, at, col_ref, *refs):
    grads = refs[: 4 * chips]
    outs = refs[4 * chips : -1]
    grad_ref = refs[-1]
    rows = grads[0].shape[0]
    half = pl.program_id(0) // (pl.num_programs(0) // 2)
    for m in range(2):

        @pl.when(half == m)
        def _():
            for n, out in enumerate(outs):
                for j in range(chips):
                    grad_ref[n, j * rows : (j + 1) * rows, :] = grads[(2 * m + n) * chips + j][...]
                out[...] = mm(col_ref[...], grad_ref[n], NN)


def weight_grads(at, cols, owns, others):
    chips = len(owns)
    rows, width = owns[0].shape
    gw = width // 2
    size = cols.shape[0]
    steps = gw // TILE
    arrays, specs = [], []
    for blocks, column in (
        (owns, lambda n: jnp.minimum(n, steps - 1)),
        (others, lambda n: jnp.maximum(n - steps, 0)),
    ):
        for half in range(2):
            for block in blocks:
                split = isinstance(block, tuple)
                first = 0 if split else half * steps
                arrays.append(block[half] if split else block)
                specs.append(pl.BlockSpec((rows, TILE), lambda n, at, f=first, c=column: (0, f + c(n))))
    out_spec = pl.BlockSpec((size, TILE), lambda n, at: (0, (n // steps ^ (at[0] & 1)) * steps + n % steps))
    return pl.pallas_call(
        functools.partial(weight_grad_kernel, chips),
        grid_spec=pltpu.PrefetchScalarGridSpec(
            num_scalar_prefetch=1,
            grid=(2 * steps,),
            in_specs=[whole(cols.shape)] + specs,
            out_specs=[out_spec] * 2,
            scratch_shapes=[pltpu.VMEM((2, chips * rows, TILE), BF16)],
        ),
        out_shape=[jax.ShapeDtypeStruct((size, width), F32)] * 2,
        compiler_params=params(16 if chips <= 4 else 28),
        cost_estimate=cost(4 * chips * rows * size * width, 2 * chips * rows * (size + 2 * width) + 8 * size * width),
    )(at, cols, *arrays)


def window_table(dp, enc_len, route, dec_len, window):
    shards = enc_len.shape[1]
    packed_rows = jnp.concatenate([enc_len, route, dec_len], axis=1)
    everyone = lax.all_to_all(
        jnp.broadcast_to(packed_rows, (shards, 3 * shards)), "dp", split_axis=0, concat_axis=0, tiled=True
    )
    lens, targets, decs = everyone[:, :shards], everyone[:, shards : 2 * shards], everyone[:, 2 * shards :]
    order = jnp.arange(shards, dtype=jnp.int32)
    before = (order[None, :] < order[:, None])[None]
    starts = jnp.sum(jnp.where(before, lens[:, None, :], 0), axis=2, dtype=jnp.int32)
    here = dp ^ jnp.arange(2, dtype=jnp.int32)
    hit = targets[None] == here[:, None, None]
    start = jnp.sum(jnp.where(hit, starts[None], 0), axis=2, dtype=jnp.int32)
    length = jnp.sum(jnp.where(hit, lens[None], 0), axis=2, dtype=jnp.int32)
    mine = jnp.sum(jnp.where((order[None] == here[:, None])[:, :, None], decs[None], 0), axis=1, dtype=jnp.int32)
    begin = jnp.sum(jnp.where(before, mine[:, None, :], 0), axis=2, dtype=jnp.int32)
    return start, length, begin


def body(queries, enc_rows, key_weight, value_weight, enc_len, dec_len, route, out_grad):
    shards = lax.axis_size("dp")
    peers = lax.axis_size("mp")
    chips = shards // 2
    packed = enc_rows.shape[0]
    window = 4 * packed // shards + 16
    gw = key_weight.shape[1] // 2
    dp, mp = lax.axis_index("dp"), lax.axis_index("mp")
    core = dp & 1
    at = jnp.stack([dp, mp]).astype(jnp.int32)

    def flip(x, r):
        return lax.ppermute(x, "dp", [(i, i ^ r) for i in range(shards)])

    def shift(x, r):
        return lax.ppermute(x, "mp", [(i, (i + r) % peers) for i in range(peers)])

    low = 1 << ((chips.bit_length() - 1) // 2)
    lows, highs = range(1, low), range(low, chips, low)

    def spread(x, low_first):
        got = {0: x}
        first, second = (lows, highs) if low_first else (highs, lows)
        for a in first:
            got[a] = flip(x, 2 * a)
        for b in second:
            got[b] = flip(x, 2 * b)
        for a in first:
            for b in second:
                got[a + b] = flip(got[a], 2 * b)
        return [got[j] for j in range(chips)]

    def collect(parts, low_first):
        first, second = (lows, highs) if low_first else (highs, lows)
        sums = {}
        for b in [*second, 0]:
            sums[b] = functools.reduce(jnp.add, [parts[b]] + [flip(parts[a + b], 2 * a) for a in first])
        return functools.reduce(jnp.add, [flip(sums[b], 2 * b) for b in second] + [sums[0]])

    def half_of(x, which):
        return lax.dynamic_slice_in_dim(x, which * gw, gw, axis=1)

    partner = flip(enc_rows, 1)
    owns = [enc_rows] + [shift(enc_rows, r) for r in range(1, peers)]
    mine, theirs = (jnp.concatenate([half_of(queries, c), half_of(out_grad, c)], axis=1) for c in (core, 1 - core))
    pair = flip(theirs, 1)
    start, length, begin = window_table(dp, enc_len, route, dec_len, window)
    base = jnp.minimum(start // 16 * 16, packed - window)
    table = jnp.stack([base, start - base, start - base + length, begin])
    sums = project(0, at, key_weight, value_weight, [enc_rows], [partner])
    sums, table, mine, pair, owns = lax.optimization_barrier((sums, table, mine, pair, owns))
    partners = [partner] + [flip(x, 1) for x in owns[1:]]
    keys, values = project(1, at, key_weight, value_weight, owns[1:], partners[1:], sums)
    keys, values = spread(keys, True), spread(values, False)
    cols = split_columns(chips, at, owns, partners)
    near = [*lows, *highs]
    far = [a + b for a in lows for b in highs]
    keys, values, cols = lax.optimization_barrier((keys, values, list(cols)))
    far_cols = [cols[j] for j in far]
    cols = [cols[0]] + [flip(cols[j], 2 * j) for j in near]
    attended, query_grad, back, *parts = attend(window, at, table, mine, pair, keys, values)
    parts, back, cols = lax.optimization_barrier((parts, back, cols))
    own = jnp.concatenate([collect(parts[:chips], False), collect(parts[chips:], True)], axis=1)
    back = flip(back, 1)
    outs = []
    for here, rest in ((attended, back[:, :gw]), (query_grad, back[:, gw:])):
        outs.append(jnp.where(core == 0, jnp.concatenate([here, rest], 1), jnp.concatenate([rest, here], 1)))
    own, cols = lax.optimization_barrier((own, cols))
    other = flip(own, 1)
    owns = {0: own}
    for j in [*lows, *highs]:
        owns[j] = flip(own, 2 * j)
    middle = peers // 2
    rest = [r for r in range(1, peers) if r != middle]
    chunks = list(project_back((middle,), peers, at, own, other, key_weight, value_weight))
    arrived = [shift(chunks[0], middle)]
    chunks += list(project_back((*rest, 0), peers, at, own, other, key_weight, value_weight))
    arrived += [shift(x, r) for x, r in zip(chunks[1:-1], rest)]
    owns, far_cols, _ = lax.optimization_barrier((owns, far_cols, chunks[:-1]))
    far_cols = [flip(x, 2 * j) for x, j in zip(far_cols, far)]
    for a in lows:
        for b in highs:
            owns[a + b] = (flip(owns[a][:, :gw], 2 * b), flip(owns[b][:, gw:], 2 * a))
    owns = [owns[j] for j in range(chips)]
    owns, arrived[:2], far_cols, chunk, outs = lax.optimization_barrier((owns, arrived[:2], far_cols, chunks[-1], outs))
    held = {j: x for j, x in zip([0] + near + far, cols + far_cols)}
    cols = jnp.concatenate([held[j] for j in range(chips)], axis=1)
    others = [other] + [tuple(flip(y, 1) for y in x) if isinstance(x, tuple) else flip(x, 1) for x in owns[1:]]
    weight_out = weight_grads(at, cols, owns, others)
    arrived, weight_out = lax.optimization_barrier((arrived, weight_out))
    total = functools.reduce(jnp.add, [x.astype(F32) for x in [chunk, *arrived]])
    return (*outs, total.T.astype(BF16), *weight_out)


def solution(mesh):
    in_specs = (
        P("dp", "mp"),
        P("dp", "mp"),
        P(None, "mp"),
        P(None, "mp"),
        P("dp", None),
        P("dp", None),
        P("dp", None),
        P("dp", "mp"),
    )
    out_specs = (P("dp", "mp"), P("dp", "mp"), P("dp", "mp"), P("dp", "mp"), P("dp", "mp"))
    return jax.shard_map(body, mesh=mesh, in_specs=in_specs, out_specs=out_specs, check_vma=False)
```

```python
import functools

import jax
import jax.numpy as jnp
from jax import lax
from jax.experimental import pallas as pl
from jax.experimental.pallas import tpu as pltpu
from jax.sharding import PartitionSpec as P

HD = 256
TILE = 256
NT = (((1,), (1,)), ((), ()))
NN = (((1,), (0,)), ((), ()))
TN = (((0,), (0,)), ((), ()))
SMEM = pl.BlockSpec(memory_space=pltpu.SMEM)
BF16 = jnp.bfloat16
F32 = jnp.float32


def mm(a, b, dims):
    return lax.dot_general(a, b, dims, preferred_element_type=F32)


def params(mib=60):
    return pltpu.CompilerParams(vmem_limit_bytes=mib * 2**20)


def cost(flops, nbytes, exps=0):
    return pl.CostEstimate(flops=flops // 1024, bytes_accessed=nbytes // 1024, transcendentals=exps // 1024)


def whole(shape):
    return pl.BlockSpec(shape, lambda *_: (0,) * len(shape))


def pair_rows(ref, core, own, partner):
    rows = own.shape[0]
    ref[pl.ds(pl.multiple_of(core * rows, rows), rows), :] = own
    ref[pl.ds(pl.multiple_of((1 - core) * rows, rows), rows), :] = partner


def project_kernel(first, blocks, cuts, final, at, kw_ref, vw_ref, *refs):
    owns, partners = refs[:blocks], refs[blocks : 2 * blocks]
    enc_ref, acc_ref, w_ref, sems = refs[-4:]
    _, steps, tile, gw = w_ref.shape
    peers = kw_ref.shape[0] // (cuts * tile)
    core = at[0] & 1
    copies = []
    for n in range(steps):
        block = lax.rem(at[1] + 2 * peers - first - n // cuts, peers)
        rows = pl.ds(pl.multiple_of((block * cuts + n % cuts) * tile, tile), tile)
        cols = pl.ds(pl.multiple_of(core * gw, gw), gw)
        for m, ref in enumerate((kw_ref, vw_ref)):
            copies.append(pltpu.make_async_copy(ref.at[rows, cols], w_ref.at[m, n], sems.at[m, n]))
            copies[-1].start()
    for n in range(steps):
        place = slice(n % cuts * tile, (n % cuts + 1) * tile)
        pair_rows(enc_ref.at[n], core, owns[n // cuts][:, place], partners[n // cuts][:, place])
    acc_ref[...] = refs[2 * blocks][...] if final else jnp.zeros_like(acc_ref)
    for n in range(steps):
        copies[2 * n].wait()
        copies[2 * n + 1].wait()
        acc_ref[:, :gw] += mm(enc_ref[n], w_ref[0, n], NN)
        acc_ref[:, gw:] += mm(enc_ref[n], w_ref[1, n], NN)
    if final:
        refs[-6][...] = acc_ref[:, :gw].astype(BF16)
        refs[-5][...] = acc_ref[:, gw:].astype(BF16)
    else:
        refs[-5][...] = acc_ref[...]


def project(first, at, key_weight, value_weight, owns, partners, sums=None):
    rows, depth = owns[0].shape
    gw = key_weight.shape[1] // 2
    blocks = len(owns)
    final = sums is not None
    cuts = 2
    tile = depth // cuts
    out_shape = (2 * rows, 2 * gw)
    half = (2 * rows, gw)
    return pl.pallas_call(
        functools.partial(project_kernel, first, blocks, cuts, final),
        grid_spec=pltpu.PrefetchScalarGridSpec(
            num_scalar_prefetch=1,
            grid=(1,),
            in_specs=[pl.BlockSpec(memory_space=pltpu.HBM)] * 2
            + [whole((rows, depth))] * (2 * blocks)
            + [whole(out_shape)] * final,
            out_specs=[whole(half)] * 2 if final else whole(out_shape),
            scratch_shapes=[
                pltpu.VMEM((blocks * cuts, 2 * rows, tile), BF16),
                pltpu.VMEM(out_shape, F32),
                pltpu.VMEM((2, blocks * cuts, tile, gw), BF16),
                pltpu.SemaphoreType.DMA((2, blocks * cuts)),
            ],
        ),
        out_shape=[jax.ShapeDtypeStruct(half, BF16)] * 2 if final else jax.ShapeDtypeStruct(out_shape, F32),
        compiler_params=params(48),
        cost_estimate=cost(8 * blocks * rows * depth * gw, 4 * blocks * depth * gw),
    )(at, key_weight, value_weight, *owns, *partners, *([sums] if final else []))


def split_kernel(peers, at, *refs):
    owns, partners = refs[:peers], refs[peers : 2 * peers]
    outs, all_ref = refs[2 * peers : -1], refs[-1]
    size = outs[0].shape[0]
    per = owns[0].shape[1] // size
    for r in range(peers):
        for c in range(per):
            place = slice(c * size, (c + 1) * size)
            pair_rows(all_ref.at[r * per + c], at[0] & 1, owns[r][:, place], partners[r][:, place])
    for j, out in enumerate(outs):
        target = at[0] ^ (2 * j)
        r = lax.rem(at[1] + peers - lax.div(target, per), peers)
        out[...] = all_ref[r * per + lax.rem(target, per)].astype(F32).T.astype(BF16)


def split_columns(chips, at, owns, partners):
    rows, depth = owns[0].shape
    peers = len(owns)
    size = peers * depth // (2 * chips)
    return pl.pallas_call(
        functools.partial(split_kernel, peers),
        grid_spec=pltpu.PrefetchScalarGridSpec(
            num_scalar_prefetch=1,
            grid=(1,),
            in_specs=[whole((rows, depth))] * (2 * peers),
            out_specs=[whole((size, 2 * rows))] * chips,
            scratch_shapes=[pltpu.VMEM((2 * chips, 2 * rows, size), BF16)],
        ),
        out_shape=[jax.ShapeDtypeStruct((size, 2 * rows), BF16)] * chips,
        compiler_params=params(16),
        cost_estimate=cost(0, 8 * peers * rows * depth),
    )(at, *owns, *partners)


def attend_kernel(chips, window, at, table, own_ref, pair_ref, *refs):
    keys, values = refs[:chips], refs[chips : 2 * chips]
    att_ref, qg_ref, back_ref = refs[2 * chips : 2 * chips + 3]
    outs = refs[2 * chips + 3 : -3]
    outs = (outs[:chips], outs[chips:])
    open_ref, key_ref, grad_ref = refs[-3:]
    rows, gw = att_ref.shape
    shards = 2 * chips
    packed = keys[0].shape[0] // 2
    keys_n = shards * window
    scale = HD ** (-0.5)
    for out in outs[0] + outs[1]:
        out[...] = jnp.zeros_like(out)
    for d in range(2):
        row = lax.broadcasted_iota(jnp.int32, (rows, 128), 0)
        low = jnp.zeros((rows, 128), jnp.int32)
        high = jnp.zeros((rows, 128), jnp.int32)
        for s in range(shards):
            place = (s ^ (at[0] & -2)) * window
            low = jnp.where(row >= table[3, d, s], place + table[1, d, s], low)
            high = jnp.where(row >= table[3, d, s], place + table[2, d, s], high)
        for c in range(0, keys_n, 128):
            col = lax.broadcasted_iota(jnp.int32, (rows, 128), 1) + c
            open_ref[d, :, c : c + 128] = jnp.where((col >= low) & (col < high), 0.0, -jnp.inf)
        bases = []
        for u in range(shards):
            bases.append(pl.multiple_of(u % 2 * packed + table[0, d, u ^ (at[0] & -2)], 16))
            key_ref[d, u * window : (u + 1) * window, :gw] = keys[u // 2][pl.ds(bases[u], window), :]
            key_ref[d, u * window : (u + 1) * window, gw:] = values[u // 2][pl.ds(bases[u], window), :]
        for h in range(gw // HD):
            mine = slice(h * HD, (h + 1) * HD)
            theirs = slice(gw + h * HD, gw + (h + 1) * HD)
            q, g = ((own_ref, pair_ref)[d][:, place] for place in (mine, theirs))
            k, v = key_ref[d, :, mine], key_ref[d, :, theirs]
            scores = mm(q, k, NT) * scale + open_ref[d]
            top = jnp.max(scores, axis=1, keepdims=True)
            expo = jnp.exp(scores - top)
            probs = expo * (1.0 / jnp.sum(expo, axis=1, keepdims=True))
            weights = probs.astype(BF16)
            attended = mm(weights, v, NN).astype(BF16)
            grad_ref[d, :, theirs] = mm(weights, g, TN).astype(BF16)
            dweights = mm(g, v, NT)
            delta = jnp.sum(probs * dweights, axis=1, keepdims=True)
            dscores = (probs * (dweights - delta) * scale).astype(BF16)
            query_grad = mm(dscores, k, NN).astype(BF16)
            grad_ref[d, :, mine] = mm(dscores, q, TN).astype(BF16)
            if d:
                back_ref[:, mine], back_ref[:, theirs] = attended, query_grad
            else:
                att_ref[:, mine], qg_ref[:, mine] = attended, query_grad
        for u in range(shards):
            for m in range(2):
                part = grad_ref[d, u * window : (u + 1) * window, m * gw : (m + 1) * gw]
                outs[m][u // 2][pl.ds(bases[u], window), :] += part


def attend(window, at, table, own, pair, keys, values):
    rows, width = own.shape
    gw = width // 2
    chips = len(keys)
    keys_n = 2 * chips * window
    half = jax.ShapeDtypeStruct((rows, gw), BF16)
    both = jax.ShapeDtypeStruct((rows, width), BF16)
    block = keys[0].shape
    return pl.pallas_call(
        functools.partial(attend_kernel, chips, window),
        grid_spec=pltpu.PrefetchScalarGridSpec(
            num_scalar_prefetch=2,
            grid=(1,),
            in_specs=[whole((rows, width))] * 2 + [whole(keys[0].shape)] * (2 * chips),
            out_specs=[whole((rows, gw))] * 2 + [whole((rows, width))] + [whole(block)] * (2 * chips),
            scratch_shapes=[
                pltpu.VMEM((2, rows, keys_n), F32),
                pltpu.VMEM((2, keys_n, width), BF16),
                pltpu.VMEM((2, keys_n, width), BF16),
            ],
        ),
        out_shape=[half, half, both] + [jax.ShapeDtypeStruct(block, BF16)] * (2 * chips),
        compiler_params=params(20 if keys_n <= 640 else 28),
        cost_estimate=cost(24 * rows * keys_n * gw, 8 * rows * width + 4 * keys_n * width, 4 * rows * keys_n),
    )(at, table, own, pair, *keys, *values)


def back_kernel(places, chunks, at, own_ref, other_ref, kw_ref, vw_ref, *refs):
    outs = refs[: len(places)]
    w_ref, turned_ref, sems = refs[len(places) :]
    depth, rows = outs[0].shape
    gw = own_ref.shape[1] // 2
    tile = min(TILE, depth)
    steps = depth // tile
    copies = []
    for c, r in enumerate(places):
        first = lax.rem(at[1] + r, chunks) * depth
        for n in range(steps):
            for m, ref in enumerate((kw_ref, vw_ref)):
                place = pl.ds(pl.multiple_of(first + n * tile, tile), tile)
                step = c * steps + n
                copies.append(pltpu.make_async_copy(ref.at[place, :], w_ref.at[m, step], sems.at[m, step]))
                copies[-1].start()
    for n, ref in enumerate((own_ref, other_ref)):
        start = pl.multiple_of(((at[0] & 1) ^ n) * gw, gw)
        for m in range(2):
            turned_ref[m, pl.ds(start, gw), :] = ref[:, m * gw : (m + 1) * gw].astype(F32).T.astype(BF16)
    for step in range(len(places) * steps):
        copies[2 * step].wait()
        copies[2 * step + 1].wait()
        total = mm(w_ref[0, step], turned_ref[0], NN) + mm(w_ref[1, step], turned_ref[1], NN)
        n = step % steps
        outs[step // steps][n * tile : (n + 1) * tile, :] = total.astype(BF16)


def project_back(places, chunks, at, own, other, key_weight, value_weight):
    rows, width = own.shape
    rows, gw = rows // 2, width // 2
    depth = key_weight.shape[0] // chunks
    tile = min(TILE, depth)
    steps = len(places) * (depth // tile)
    row_spec = pl.BlockSpec((rows, width), lambda n, at: (at[0] & 1, 0))
    return pl.pallas_call(
        functools.partial(back_kernel, places, chunks),
        grid_spec=pltpu.PrefetchScalarGridSpec(
            num_scalar_prefetch=1,
            grid=(1,),
            in_specs=[row_spec] * 2 + [pl.BlockSpec(memory_space=pltpu.HBM)] * 2,
            out_specs=[whole((depth, rows))] * len(places),
            scratch_shapes=[
                pltpu.VMEM((2, steps, tile, 2 * gw), BF16),
                pltpu.VMEM((2, 2 * gw, rows), BF16),
                pltpu.SemaphoreType.DMA((2, steps)),
            ],
        ),
        out_shape=[jax.ShapeDtypeStruct((depth, rows), BF16)] * len(places),
        compiler_params=params(48),
        cost_estimate=cost(8 * rows * gw * depth, 8 * gw * depth),
    )(at, own, other, key_weight, value_weight)


def weight_grad_kernel(chips, at, col_ref, *refs):
    grads = refs[: 4 * chips]
    outs = refs[4 * chips : -1]
    grad_ref = refs[-1]
    rows = grads[0].shape[0]
    half = pl.program_id(0) // (pl.num_programs(0) // 2)
    for m in range(2):

        @pl.when(half == m)
        def _():
            for n, out in enumerate(outs):
                for j in range(chips):
                    grad_ref[n, j * rows : (j + 1) * rows, :] = grads[(2 * m + n) * chips + j][...]
                out[...] = mm(col_ref[...], grad_ref[n], NN)


def weight_grads(at, cols, owns, others):
    chips = len(owns)
    rows, width = owns[0].shape
    gw = width // 2
    size = cols.shape[0]
    steps = gw // TILE
    arrays, specs = [], []
    for blocks, column in (
        (owns, lambda n: jnp.minimum(n, steps - 1)),
        (others, lambda n: jnp.maximum(n - steps, 0)),
    ):
        for half in range(2):
            for block in blocks:
                split = isinstance(block, tuple)
                first = 0 if split else half * steps
                arrays.append(block[half] if split else block)
                specs.append(pl.BlockSpec((rows, TILE), lambda n, at, f=first, c=column: (0, f + c(n))))
    out_spec = pl.BlockSpec((size, TILE), lambda n, at: (0, (n // steps ^ (at[0] & 1)) * steps + n % steps))
    return pl.pallas_call(
        functools.partial(weight_grad_kernel, chips),
        grid_spec=pltpu.PrefetchScalarGridSpec(
            num_scalar_prefetch=1,
            grid=(2 * steps,),
            in_specs=[whole(cols.shape)] + specs,
            out_specs=[out_spec] * 2,
            scratch_shapes=[pltpu.VMEM((2, chips * rows, TILE), BF16)],
        ),
        out_shape=[jax.ShapeDtypeStruct((size, width), F32)] * 2,
        compiler_params=params(16 if chips <= 4 else 28),
        cost_estimate=cost(4 * chips * rows * size * width, 2 * chips * rows * (size + 2 * width) + 8 * size * width),
    )(at, cols, *arrays)


def window_table(dp, enc_len, route, dec_len, window):
    shards = enc_len.shape[1]
    packed_rows = jnp.concatenate([enc_len, route, dec_len], axis=1)
    everyone = lax.all_to_all(
        jnp.broadcast_to(packed_rows, (shards, 3 * shards)), "dp", split_axis=0, concat_axis=0, tiled=True
    )
    lens, targets, decs = everyone[:, :shards], everyone[:, shards : 2 * shards], everyone[:, 2 * shards :]
    order = jnp.arange(shards, dtype=jnp.int32)
    before = (order[None, :] < order[:, None])[None]
    starts = jnp.sum(jnp.where(before, lens[:, None, :], 0), axis=2, dtype=jnp.int32)
    here = dp ^ jnp.arange(2, dtype=jnp.int32)
    hit = targets[None] == here[:, None, None]
    start = jnp.sum(jnp.where(hit, starts[None], 0), axis=2, dtype=jnp.int32)
    length = jnp.sum(jnp.where(hit, lens[None], 0), axis=2, dtype=jnp.int32)
    mine = jnp.sum(jnp.where((order[None] == here[:, None])[:, :, None], decs[None], 0), axis=1, dtype=jnp.int32)
    begin = jnp.sum(jnp.where(before, mine[:, None, :], 0), axis=2, dtype=jnp.int32)
    return start, length, begin


def body(queries, enc_rows, key_weight, value_weight, enc_len, dec_len, route, out_grad):
    shards = lax.axis_size("dp")
    peers = lax.axis_size("mp")
    chips = shards // 2
    packed = enc_rows.shape[0]
    window = 4 * packed // shards + 16
    gw = key_weight.shape[1] // 2
    dp, mp = lax.axis_index("dp"), lax.axis_index("mp")
    core = dp & 1
    at = jnp.stack([dp, mp]).astype(jnp.int32)

    def flip(x, r):
        return lax.ppermute(x, "dp", [(i, i ^ r) for i in range(shards)])

    def shift(x, r):
        return lax.ppermute(x, "mp", [(i, (i + r) % peers) for i in range(peers)])

    low = 1 << ((chips.bit_length() - 1) // 2)
    lows, highs = range(1, low), range(low, chips, low)

    def spread(x, low_first):
        got = {0: x}
        first, second = (lows, highs) if low_first else (highs, lows)
        for a in first:
            got[a] = flip(x, 2 * a)
        for b in second:
            got[b] = flip(x, 2 * b)
        for a in first:
            for b in second:
                got[a + b] = flip(got[a], 2 * b)
        return [got[j] for j in range(chips)]

    def collect(parts, low_first):
        first, second = (lows, highs) if low_first else (highs, lows)
        sums = {}
        for b in [*second, 0]:
            sums[b] = functools.reduce(jnp.add, [parts[b]] + [flip(parts[a + b], 2 * a) for a in first])
        return functools.reduce(jnp.add, [flip(sums[b], 2 * b) for b in second] + [sums[0]])

    def half_of(x, which):
        return lax.dynamic_slice_in_dim(x, which * gw, gw, axis=1)

    partner = flip(enc_rows, 1)
    owns = [enc_rows] + [shift(enc_rows, r) for r in range(1, peers)]
    mine, theirs = (jnp.concatenate([half_of(queries, c), half_of(out_grad, c)], axis=1) for c in (core, 1 - core))
    pair = flip(theirs, 1)
    start, length, begin = window_table(dp, enc_len, route, dec_len, window)
    base = jnp.minimum(start // 16 * 16, packed - window)
    table = jnp.stack([base, start - base, start - base + length, begin])
    sums = project(0, at, key_weight, value_weight, [enc_rows], [partner])
    sums, table, mine, pair, owns = lax.optimization_barrier((sums, table, mine, pair, owns))
    partners = [partner] + [flip(x, 1) for x in owns[1:]]
    keys, values = project(1, at, key_weight, value_weight, owns[1:], partners[1:], sums)
    keys, values = spread(keys, True), spread(values, False)
    cols = split_columns(chips, at, owns, partners)
    near = [*lows, *highs]
    far = [a + b for a in lows for b in highs]
    keys, values, cols = lax.optimization_barrier((keys, values, list(cols)))
    far_cols = [cols[j] for j in far]
    cols = [cols[0]] + [flip(cols[j], 2 * j) for j in near]
    attended, query_grad, back, *parts = attend(window, at, table, mine, pair, keys, values)
    parts, back, cols = lax.optimization_barrier((parts, back, cols))
    own = jnp.concatenate([collect(parts[:chips], False), collect(parts[chips:], True)], axis=1)
    back = flip(back, 1)
    outs = []
    for here, rest in ((attended, back[:, :gw]), (query_grad, back[:, gw:])):
        outs.append(jnp.where(core == 0, jnp.concatenate([here, rest], 1), jnp.concatenate([rest, here], 1)))
    own, cols, far_cols = lax.optimization_barrier((own, cols, far_cols))
    far_cols = [flip(x, 2 * j) for x, j in zip(far_cols, far)]
    other = flip(own, 1)
    owns = {0: own}
    for j in [*lows, *highs]:
        owns[j] = flip(own, 2 * j)
    middle = peers // 2
    rest = [r for r in range(1, peers) if r != middle]
    chunks = list(project_back((middle,), peers, at, own, other, key_weight, value_weight))
    arrived = [shift(chunks[0], middle)]
    chunks += list(project_back((*rest, 0), peers, at, own, other, key_weight, value_weight))
    arrived += [shift(x, r) for x, r in zip(chunks[1:-1], rest)]
    owns, far_cols, _ = lax.optimization_barrier((owns, far_cols, chunks[:-1]))
    for a in lows:
        for b in highs:
            owns[a + b] = (flip(owns[a][:, :gw], 2 * b), flip(owns[b][:, gw:], 2 * a))
    owns = [owns[j] for j in range(chips)]
    owns, arrived[:2], chunk, outs = lax.optimization_barrier((owns, arrived[:2], chunks[-1], outs))
    held = {j: x for j, x in zip([0] + near + far, cols + far_cols)}
    cols = jnp.concatenate([held[j] for j in range(chips)], axis=1)
    others = [other] + [tuple(flip(y, 1) for y in x) if isinstance(x, tuple) else flip(x, 1) for x in owns[1:]]
    weight_out = weight_grads(at, cols, owns, others)
    arrived, weight_out = lax.optimization_barrier((arrived, weight_out))
    total = functools.reduce(jnp.add, [x.astype(F32) for x in [chunk, *arrived]])
    return (*outs, total.T.astype(BF16), *weight_out)


def solution(mesh):
    in_specs = (
        P("dp", "mp"),
        P("dp", "mp"),
        P(None, "mp"),
        P(None, "mp"),
        P("dp", None),
        P("dp", None),
        P("dp", None),
        P("dp", "mp"),
    )
    out_specs = (P("dp", "mp"), P("dp", "mp"), P("dp", "mp"), P("dp", "mp"), P("dp", "mp"))
    return jax.shard_map(body, mesh=mesh, in_specs=in_specs, out_specs=out_specs, check_vma=False)
```
